1024 devices in a mesh: expert: 16 (over y, x_hi, core), replica: 64 (over x_lo, z).
Axes of the slice: x: 4 (x_hi: 2, x_lo: 2; x = x_hi * 2 + x_lo), y: 4, z: 32, core: 2. Of those that a mesh axis runs over, the one named last changes fastest.
Arguments:
- tokens: bfloat16 [2048, 4096], P('replica', 'expert'), may hold values from -6 to 6
- cotangent: bfloat16 [2048, 4096], P('replica', 'expert'), may hold values from -6 to 6
- route_probs: float32 [2048, 8], P('replica'), may hold values from 0.05 to 0.3
- expert_ids: int32 [2048, 8], P('replica'), may hold values from 0 to 63, all different within a row; in each aligned block of 32 rows (0 to 31, 32 to 63, ...) at most 8 rows name the same one
- seq_ids: int32 [2048], P('replica'), may hold values from 0 to 255, never falling along the last dimension, each value on 1 to 16 neighbouring positions
- ratios: float32 [256], replicated, may hold values from 0.5 to 2
- gate_weight: bfloat16 [64, 4096, 1024], P('replica', 'expert'), may hold values from -0.09375 to 0.09375
- up_weight: bfloat16 [64, 4096, 1024], P('replica', 'expert'), may hold values from -0.09375 to 0.09375
- down_weight: bfloat16 [64, 1024, 4096], P('replica', None, 'expert'), may hold values from -0.1875 to 0.1875
Outputs:
- layer_out: bfloat16 [2048, 4096], P('replica', 'expert')
- grad_tokens: bfloat16 [2048, 4096], P('replica', 'expert')
- grad_gate: bfloat16 [64, 4096, 1024], P('replica', 'expert')
- grad_up: bfloat16 [64, 4096, 1024], P('replica', 'expert')
- grad_down: bfloat16 [64, 1024, 4096], P('replica', None, 'expert')
The draws below stay inside these ranges and needn't reach their ends.
Inputs may be any that keep to these rules, and one draw needn't show every extreme that they name: `expert_ids`: each token names 8 different experts. Within the 32 tokens of one device (aligned blocks of the token order), no expert is named by more than 8 tokens, a bound that some block reaches. `seq_ids`: never falls along the token order; a sequence holds at most 16 tokens, and some sequence exactly 16.
All inputs are finite; a program needn't handle non-finite values.
Results may differ from the reference program's by a relative error of at most 0.035.
Values may be sent and summed in bfloat16 or wider, within the bound.
No kernel may reach another device: no remote copies, remote signals or barrier semaphores. Data moves between devices by JAX's collectives and lax.ppermute only.
A program may use at most 32 MiB of HBM per device.

```python
import math
import jax
import jax.numpy as jnp
import numpy as np
from jax import lax

D = 4096
H = 1024
EXPERTS = 64
TOP = 8
TOK_DEV = 32
CAP = 8
TOKENS = 2048
SEQS = 256
N_EXPERT = 16
N_REPLICA = 64


def levels(rng, extent, cuts, least, high):
    gain = 1.0
    for position, shards_of in cuts:
        draws = jax.random.uniform(jax.random.fold_in(jax.random.fold_in(rng, 6), position), (shards_of,), jnp.float32, least / len(cuts), high / len(cuts))
        gain = gain * jnp.repeat(jnp.exp(draws), extent[position] // shards_of).reshape((-1,) + (1,) * (len(extent) - 1 - position))
    return gain


def split_up(amount, total, limit, lean):
    loads = [(1 << 20) // math.isqrt(rank ** lean) + 1 for rank in range(2, amount + 1)]
    spare, counts = total - limit - (amount - 1), [1] * (amount - 1)
    while spare > 0:
        candidates = [i for i in range(amount - 1) if counts[i] < limit]
        mass, left = sum([loads[i] for i in candidates]), spare
        for i in candidates:
            more = min(limit - counts[i], max(1, left * loads[i] // mass), spare)
            counts[i] = counts[i] + more
            spare = spare - more
    return np.array([limit] + counts)


def ragged(stream_key, number_of, total, bound, skew):
    if number_of == 2:
        one = jax.random.randint(stream_key, (), max(1, total - bound), min(bound, total - 1) + 1)
        return jnp.stack([one, total - one])
    tallies = jnp.asarray(split_up(number_of, total, bound, skew), jnp.int32)
    pairs = (number_of - 1) // 2
    donor, receiver = tallies[1:1 + 2 * pairs:2], tallies[2:2 + 2 * pairs:2]
    room = jnp.minimum(donor - 1, bound - receiver)
    passed = jax.random.randint(jax.random.fold_in(stream_key, 1), (pairs,), 0, 1 << 20) % (room + 1)
    tallies = tallies.at[1:1 + 2 * pairs:2].set(donor - passed).at[2:2 + 2 * pairs:2].set(receiver + passed)
    return tallies[jax.random.permutation(jax.random.fold_in(stream_key, 2), number_of)]


def assign_block(rng, own, number, rows, amount, top, reach, skew):
    sequence = jax.random.permutation(rng, amount)
    crowded, ordinary = load_shares(amount, rows * top, reach, skew, True), load_shares(amount, rows * top, reach, skew, False)
    places = jnp.arange(amount)

    def named(lengths, turn):
        used = int((lengths > 0).sum())
        fixed = max(1, used // 4)
        passed = fixed + (places - fixed + turn * (used - fixed)) % max(1, amount - fixed)
        return jnp.zeros((amount,), jnp.int32).at[sequence[jnp.where(places < fixed, places, passed)]].set(jnp.asarray(lengths, jnp.int32))

    lengths = jnp.where(number % 4 == 0, named(crowded, number // 4), named(ordinary, number - number // 4 - 1))
    mixed = jax.random.permutation(jax.random.fold_in(own, 3), amount)
    donor, receiver = mixed[0:amount // 2 * 2:2], mixed[1:amount // 2 * 2:2]
    room = jnp.minimum(lengths[donor] - 1, reach - lengths[receiver]) // 2
    room = jnp.where((donor == sequence[0]) | (receiver == sequence[0]) | (lengths[receiver] == 0), 0, jnp.maximum(room, 0))
    passed = jax.random.randint(jax.random.fold_in(own, 4), (amount // 2,), 0, 1 << 20) % (room + 1)
    lengths = lengths.at[donor].add(-passed).at[receiver].add(passed)
    items = jnp.searchsorted(jnp.cumsum(lengths), jnp.arange(rows * top), side="right").astype(jnp.int32)
    listing = items.reshape(top, rows).T
    listing = listing[jax.random.permutation(jax.random.fold_in(own, 1), rows)]
    turn = jax.random.randint(jax.random.fold_in(own, 2), (rows, 1), 0, top)
    return jnp.take_along_axis(listing, (jnp.arange(top)[None, :] + turn) % top, axis=1)


def load_shares(number_of, total, bound, skew, full):
    loads = [(1 << 20) // math.isqrt(grade ** skew) + 1 for grade in range(1, number_of + 1)]
    largest = bound if full else min(bound, max(-(-total // number_of), total * loads[0] // sum(loads)))
    least = 1 if total - largest >= number_of - 1 else 0
    given, surplus = [largest] + [least] * (number_of - 1), total - largest - least * (number_of - 1)
    while surplus > 0:
        candidates = [i for i in range(1, number_of) if given[i] < largest] or [i for i in range(1, number_of) if given[i] < bound]
        whole, remaining = sum([loads[i] for i in candidates]), surplus
        for i in candidates:
            addition = min(bound - given[i], max(1, remaining * loads[i] // whole), surplus)
            given[i] = given[i] + addition
            surplus = surplus - addition
    return np.array(given)


def gaussian(stream_key, dims, scale, reach, split=(), kind=jnp.bfloat16):
    level = levels(stream_key, dims, split, -0.22, 0.18) if split else 1.0
    result = jax.random.normal(stream_key, dims, jnp.float32) * scale * level
    return jnp.minimum(jnp.maximum(result, -reach), reach).astype(kind)


def setup_inputs(seed: int = 0) -> dict:
    keys = jax.random.split(jax.random.key(seed), 10)
    tokens = gaussian(keys[0], (TOKENS, D), 1.0, 6.0, ((0, 64), (1, 16)))
    cotangent = gaussian(keys[1], (TOKENS, D), 1.0, 6.0, ((0, 64), (1, 16)))
    route_probs = jnp.clip(0.05 + 0.25 * jax.random.uniform(keys[2], (TOKENS, TOP), jnp.float32) ** levels(keys[2], (TOKENS, TOP), ((0, 64),), -0.2, 0.2), 0.05, 0.3)
    expert_ids_keys = jax.random.split(jax.random.fold_in(keys[3], 1), TOKENS // TOK_DEV)
    expert_ids_turns = jax.random.permutation(jax.random.fold_in(keys[3], 3), TOKENS // TOK_DEV)
    expert_ids = jax.vmap(lambda own, number: assign_block(jax.random.fold_in(keys[3], 2), own, number, TOK_DEV, EXPERTS, TOP, CAP, 2))(expert_ids_keys, expert_ids_turns).reshape((TOKENS, TOP))
    seq_ids = jnp.searchsorted(jnp.cumsum(ragged(keys[4], SEQS, TOKENS, 16, 2)), jnp.arange(TOKENS), side="right").astype(jnp.int32)
    ratios = jnp.clip(jnp.exp(jax.random.uniform(keys[5], (SEQS,), jnp.float32, math.log(0.5), math.log(2.0))), 0.5, 2.0)
    gate_weight = gaussian(keys[6], (EXPERTS, D, H), D ** -0.5, 0.09375, ((0, 64), (1, 16)))
    up_weight = gaussian(keys[7], (EXPERTS, D, H), D ** -0.5, 0.09375, ((0, 64), (1, 16)))
    down_weight = gaussian(keys[8], (EXPERTS, H, D), H ** -0.5, 0.1875, ((0, 64), (2, 16)))
    return dict(tokens=tokens, cotangent=cotangent, route_probs=route_probs, expert_ids=expert_ids, seq_ids=seq_ids, ratios=ratios, gate_weight=gate_weight, up_weight=up_weight, down_weight=down_weight)


clip_low = 0.8
clip_high = 1.25


def silu_parts(gate_sum):
    sigmoid = jax.nn.sigmoid(gate_sum)
    return gate_sum * sigmoid, sigmoid * (1.0 + gate_sum * (1.0 - sigmoid))


def group_sum(partials):
    rounded = partials.astype(jnp.bfloat16)
    rounded = lax.optimization_barrier(rounded)
    return jnp.sum(rounded.astype(jnp.float32), axis=0)


def expert_pass(operands):
    inputs, seed_rows, gate_weight, up_weight, down_weight = operands
    slot_rows = inputs.shape[0]
    group_width = D // N_EXPERT
    grouped = inputs.astype(jnp.float32).reshape(slot_rows, N_EXPERT, group_width)
    gate_groups = gate_weight.astype(jnp.float32).reshape(N_EXPERT, group_width, H)
    up_groups = up_weight.astype(jnp.float32).reshape(N_EXPERT, group_width, H)
    gate_sum = group_sum(jnp.einsum("rjd,jdh->jrh", grouped, gate_groups))
    up_sum = group_sum(jnp.einsum("rjd,jdh->jrh", grouped, up_groups))
    active, slopes = silu_parts(gate_sum)
    hidden = (active * up_sum).astype(jnp.bfloat16)
    outputs = jnp.dot(hidden, down_weight, preferred_element_type=jnp.float32).astype(jnp.bfloat16)
    seed_groups = seed_rows.astype(jnp.float32).reshape(slot_rows, N_EXPERT, group_width)
    down_groups = down_weight.astype(jnp.float32).reshape(H, N_EXPERT, group_width)
    hidden_cot = group_sum(jnp.einsum("rjd,hjd->jrh", seed_groups, down_groups))
    gate_cot = (hidden_cot * up_sum * slopes).astype(jnp.bfloat16)
    up_cot = (hidden_cot * active).astype(jnp.bfloat16)
    back_rows = (jnp.dot(gate_cot, gate_weight.T, preferred_element_type=jnp.float32)
                 + jnp.dot(up_cot, up_weight.T, preferred_element_type=jnp.float32)).astype(jnp.bfloat16)
    grad_gate = jnp.dot(inputs.T, gate_cot, preferred_element_type=jnp.float32).astype(jnp.bfloat16)
    grad_up = jnp.dot(inputs.T, up_cot, preferred_element_type=jnp.float32).astype(jnp.bfloat16)
    grad_down = jnp.dot(hidden.T, seed_rows, preferred_element_type=jnp.float32).astype(jnp.bfloat16)
    return outputs, back_rows, grad_gate, grad_up, grad_down


def reference(tokens, cotangent, route_probs, expert_ids, seq_ids, ratios, gate_weight, up_weight, down_weight):
    slot_rows = N_REPLICA * CAP
    blocks = expert_ids.reshape(N_REPLICA, TOK_DEV, TOP)
    labels = jnp.arange(EXPERTS, dtype=jnp.int32)
    member = jnp.sum((blocks[..., None] == labels).astype(jnp.int32), axis=2)
    before = jnp.cumsum(member, axis=1) - member
    slot_index = jnp.take_along_axis(before, blocks, axis=2).reshape(TOKENS, TOP)
    block_index = (jnp.arange(TOKENS, dtype=jnp.int32) // TOK_DEV)[:, None]
    target = (expert_ids * slot_rows + block_index * CAP + slot_index).reshape(-1).astype(jnp.int32)
    weights = jnp.clip(ratios[seq_ids], clip_low, clip_high)
    scaled = ((route_probs * weights[:, None])[:, :, None] * cotangent.astype(jnp.float32)[:, None, :]).astype(jnp.bfloat16)
    repeated = jnp.broadcast_to(tokens[:, None, :], (TOKENS, TOP, D))
    inputs = jnp.zeros((EXPERTS * slot_rows, D), jnp.bfloat16).at[target].set(repeated.reshape(-1, D))
    inputs = inputs.reshape(EXPERTS, slot_rows, D)
    seed_rows = jnp.zeros((EXPERTS * slot_rows, D), jnp.bfloat16).at[target].set(scaled.reshape(-1, D))
    seed_rows = seed_rows.reshape(EXPERTS, slot_rows, D)
    outputs, back_rows, grad_gate, grad_up, grad_down = lax.map(
        expert_pass, (inputs, seed_rows, gate_weight, up_weight, down_weight))
    out_routes = outputs.reshape(EXPERTS * slot_rows, D)[target].reshape(TOKENS, TOP, D).astype(jnp.float32)
    layer_out = jnp.sum(route_probs[:, :, None] * out_routes, axis=1).astype(jnp.bfloat16)
    back_routes = back_rows.reshape(EXPERTS * slot_rows, D)[target].reshape(TOKENS, TOP, D).astype(jnp.float32)
    grad_tokens = jnp.sum(back_routes, axis=1).astype(jnp.bfloat16)
    return layer_out, grad_tokens, grad_gate, grad_up, grad_down
```

```python
import jax
import jax.numpy as jnp
from jax import lax
from jax.experimental import pallas as pl
from jax.experimental.pallas import tpu as pltpu
from jax.sharding import PartitionSpec as P

clip_low = 0.8
clip_high = 1.25

bf16 = jnp.bfloat16
f32 = jnp.float32

NN = (((1,), (0,)), ((), ()))
NT = (((1,), (1,)), ((), ()))
TN = (((0,), (0,)), ((), ()))


def mm(a, b, dims):
    return lax.dot_general(a, b, dims, preferred_element_type=f32)


def call(body, outs, flops, nbytes, **more):
    return pl.pallas_call(
        body,
        out_shape=outs,
        cost_estimate=pl.CostEstimate(flops=flops, bytes_accessed=nbytes, transcendentals=0),
        compiler_params=pltpu.CompilerParams(vmem_limit_bytes=40 * 1024 * 1024),
        **more,
    )


def pieces(x):
    first = x.astype(bf16)
    rest = x - first.astype(f32)
    second = rest.astype(bf16)
    third = (rest - second.astype(f32)).astype(bf16)
    return jnp.concatenate([first, second, third], axis=0)


def pack_kernel(tokens_ref, cot_ref, probs_ref, ids_ref, seq_ref, ratios_ref, send_ref, table_ref):
    count, width = tokens_ref.shape
    routes = ids_ref.shape[1]
    places = send_ref.shape[0]
    capacity = 8
    rows = lax.broadcasted_iota(jnp.int32, (count, count), 0)
    cols = lax.broadcasted_iota(jnp.int32, (count, count), 1)
    seq_row = seq_ref[...].astype(f32)
    seq_col = jnp.sum(jnp.where(rows == cols, seq_row, 0.0), axis=1, keepdims=True)
    labels = lax.broadcasted_iota(jnp.int32, (count, ratios_ref.shape[1]), 1).astype(f32)
    picked = jnp.sum(jnp.where(labels == seq_col, ratios_ref[...], 0.0), axis=1, keepdims=True)
    weights = jnp.clip(picked, clip_low, clip_high)
    probs = probs_ref[...]
    scaled = probs * weights
    ids = ids_ref[...]
    place = lax.broadcasted_iota(jnp.int32, (count, places), 1)
    owner = place // capacity
    member = jnp.zeros((count, places), f32)
    prob_at = jnp.zeros((count, places), f32)
    scale_at = jnp.zeros((count, places), f32)
    for k in range(routes):
        named = ids[:, k : k + 1] == owner
        member = jnp.where(named, 1.0, member)
        prob_at = jnp.where(named, probs[:, k : k + 1], prob_at)
        scale_at = jnp.where(named, scaled[:, k : k + 1], scale_at)
    lower = jnp.where(rows > cols, 1.0, 0.0).astype(bf16)
    before = mm(lower, member.astype(bf16), NN)
    here = (member > 0.0) & (before == (place % capacity).astype(f32))
    table = jnp.where(here, 1.0, 0.0).astype(bf16)
    table_ref[0 : 3 * count, :] = pieces(jnp.where(here, prob_at, 0.0))
    table_ref[3 * count : 4 * count, :] = table
    cot = cot_ref[...]
    send_ref[:, 0:width] = mm(table, tokens_ref[...], TN).astype(bf16)
    seeds = mm(
        pieces(jnp.where(here, scale_at, 0.0)), jnp.concatenate([cot, cot, cot], axis=0), TN
    )
    send_ref[:, width : 2 * width] = seeds.astype(bf16)


def partial_kernel(flip, rows_ref, gate_ref, up_ref, down_ref, out_ref):
    half = out_ref.shape[0]
    width = gate_ref.shape[0]
    hidden = gate_ref.shape[1]
    side = (lax.axis_index("expert") + flip) % 2
    at = pl.ds(pl.multiple_of(side * half, half), half)
    inputs = rows_ref[at, 0:width]
    seeds = rows_ref[at, width : 2 * width]
    out_ref[:, 0:hidden] = mm(inputs, gate_ref[...], NN).astype(bf16)
    out_ref[:, hidden : 2 * hidden] = mm(inputs, up_ref[...], NN).astype(bf16)
    out_ref[:, 2 * hidden : 3 * hidden] = mm(seeds, down_ref[...], NT).astype(bf16)


def add_kernel(a_ref, b_ref, out_ref):
    out_ref[...] = (a_ref[...].astype(f32) + b_ref[...].astype(f32)).astype(bf16)


def middle_kernel(parts_ref, out_ref):
    groups, rows, wide = parts_ref.shape
    hidden = wide // 3
    total = parts_ref[0].astype(f32)
    for g in range(1, groups):
        total = total + parts_ref[g].astype(f32)
    gate_sum = total[:, 0:hidden]
    up_sum = total[:, hidden : 2 * hidden]
    hidden_cot = total[:, 2 * hidden : 3 * hidden]
    sigmoid = 1.0 / (1.0 + jnp.exp(-gate_sum))
    active = gate_sum * sigmoid
    slopes = sigmoid * (1.0 + gate_sum * (1.0 - sigmoid))
    inner = (active * up_sum).astype(bf16)
    gate_cot = (hidden_cot * up_sum * slopes).astype(bf16)
    up_cot = (hidden_cot * active).astype(bf16)
    for g in range(groups):
        out_ref[g, :, 0:hidden] = inner
        out_ref[g, :, hidden : 2 * hidden] = gate_cot
        out_ref[g, :, 2 * hidden : 3 * hidden] = up_cot


def back_half(hgu_ref, gate_ref, up_ref, down_ref):
    hidden = gate_ref.shape[1]
    out = mm(hgu_ref[:, 0:hidden], down_ref[...], NN).astype(bf16)
    back = mm(hgu_ref[:, hidden : 2 * hidden], gate_ref[...], NT) + mm(
        hgu_ref[:, 2 * hidden : 3 * hidden], up_ref[...], NT
    )
    return out, back.astype(bf16)


def own_back_kernel(hgu_ref, gate_ref, up_ref, down_ref, out_ref):
    width = gate_ref.shape[0]
    out, back = back_half(hgu_ref, gate_ref, up_ref, down_ref)
    out_ref[:, 0:width] = out
    out_ref[:, width : 2 * width] = back


def other_back_kernel(own_ref, hgu_ref, gate_ref, up_ref, down_ref, out_ref):
    width = gate_ref.shape[0]
    half = own_ref.shape[0]
    core = lax.axis_index("expert") % 2
    mine = pl.ds(pl.multiple_of(core * half, half), half)
    theirs = pl.ds(pl.multiple_of((1 - core) * half, half), half)
    out_ref[mine, :] = own_ref[...]
    out, back = back_half(hgu_ref, gate_ref, up_ref, down_ref)
    out_ref[theirs, 0:width] = out
    out_ref[theirs, width : 2 * width] = back


def grads_kernel(rows_ref, own_ref, other_ref, grad_gate_ref, grad_up_ref, grad_down_ref):
    width, hidden = grad_gate_ref.shape
    half = own_ref.shape[0]
    core = lax.axis_index("expert") % 2
    mine = pl.ds(pl.multiple_of(core * half, half), half)
    theirs = pl.ds(pl.multiple_of((1 - core) * half, half), half)

    def both(columns, hgu):
        return mm(rows_ref[mine, columns], own_ref[:, hgu], TN) + mm(
            rows_ref[theirs, columns], other_ref[:, hgu], TN
        )

    inputs = slice(0, width)
    seeds = slice(width, 2 * width)
    grad_gate_ref[...] = both(inputs, slice(hidden, 2 * hidden)).astype(bf16)
    grad_up_ref[...] = both(inputs, slice(2 * hidden, 3 * hidden)).astype(bf16)
    inner = slice(0, hidden)
    grad_down_ref[...] = (
        mm(own_ref[:, inner], rows_ref[mine, seeds], TN)
        + mm(other_ref[:, inner], rows_ref[theirs, seeds], TN)
    ).astype(bf16)


def combine_kernel(table_ref, came_ref, out_ref, grad_ref):
    count, width = out_ref.shape
    parts = mm(table_ref[0 : 3 * count, :], came_ref[:, 0:width], NN)
    out_ref[...] = (
        parts[0:count] + parts[count : 2 * count] + parts[2 * count : 3 * count]
    ).astype(bf16)
    grad_ref[...] = mm(
        table_ref[3 * count : 4 * count, :], came_ref[:, width : 2 * width], NN
    ).astype(bf16)


def local(
    tokens, cotangent, route_probs, expert_ids, seq_ids, ratios, gate_weight, up_weight, down_weight
):
    count, width = tokens.shape
    hidden = gate_weight.shape[2]
    sources = lax.axis_size("replica")
    groups = lax.axis_size("expert")
    capacity = count // 4
    places = sources * capacity
    half = places // 2
    gate, up, down = gate_weight[0], up_weight[0], down_weight[0]
    shape = jax.ShapeDtypeStruct
    swap = [(i, i ^ 1) for i in range(groups)]
    sides = [list(range(0, groups, 2)), list(range(1, groups, 2))]
    product = 2 * half * width * hidden

    def spread(x, axis, index_groups=None):
        return lax.all_to_all(
            x, axis, split_axis=0, concat_axis=0, axis_index_groups=index_groups, tiled=True
        )

    send, table = call(
        pack_kernel,
        (shape((places, 2 * width), bf16), shape((4 * count, places), bf16)),
        2 * places * 4 * count * width,
        2 * places * 2 * width,
    )(
        tokens,
        cotangent,
        route_probs,
        expert_ids,
        seq_ids.reshape(1, count),
        ratios.reshape(1, -1),
    )
    rows = spread(send.reshape(sources, capacity, 2 * width), "replica").reshape(places, 2 * width)

    def partial(flip):
        return call(
            lambda *refs: partial_kernel(flip, *refs),
            shape((half, 3 * hidden), bf16),
            3 * product,
            2 * (half * 3 * hidden + 3 * width * hidden),
        )(rows, gate, up, down)

    came = lax.ppermute(partial(1), "expert", swap)
    mine = partial(0)
    summed = call(
        add_kernel, shape((half, 3 * hidden), bf16), half * 3 * hidden, 6 * half * 3 * hidden
    )(mine, came)
    eighth = half // (groups // 2)
    parts = spread(summed.reshape(groups // 2, eighth, 3 * hidden), "expert", sides)
    copies = call(
        middle_kernel,
        shape((groups // 2, eighth, 3 * hidden), bf16),
        20 * half * 3 * hidden,
        4 * half * 3 * hidden,
    )(parts)
    own = spread(copies, "expert", sides).reshape(half, 3 * hidden)
    other = lax.ppermute(own, "expert", swap)
    own_back = call(
        own_back_kernel, shape((half, 2 * width), bf16), 3 * product, 2 * 3 * width * hidden
    )(own, gate, up, down)
    back = call(
        other_back_kernel, shape((places, 2 * width), bf16), 3 * product, 2 * 3 * width * hidden
    )(own_back, other, gate, up, down)
    returned = spread(back.reshape(sources, capacity, 2 * width), "replica")
    grads = call(
        grads_kernel,
        (
            shape((width, hidden), bf16),
            shape((width, hidden), bf16),
            shape((hidden, width), bf16),
        ),
        6 * product,
        2 * 12 * width * hidden,
    )(rows, own, other)
    layer_out, grad_tokens = call(
        combine_kernel,
        (shape((count, width), bf16), shape((count, width), bf16)),
        2 * places * 4 * count * width,
        2 * places * 2 * width,
    )(table, returned.reshape(places, 2 * width))
    return (layer_out, grad_tokens) + tuple(g[None] for g in grads)


def solution(mesh):
    return jax.shard_map(
        local,
        mesh=mesh,
        in_specs=(
            P("replica", "expert"),
            P("replica", "expert"),
            P("replica", None),
            P("replica", None),
            P("replica"),
            P(),
            P("replica", "expert", None),
            P("replica", "expert", None),
            P("replica", None, "expert"),
        ),
        out_specs=(
            P("replica", "expert"),
            P("replica", "expert"),
            P("replica", "expert", None),
            P("replica", "expert", None),
            P("replica", None, "expert"),
        ),
        check_vma=False,
    )
```

```python
import jax
import jax.numpy as jnp
from jax import lax
from jax.experimental import pallas as pl
from jax.experimental.pallas import tpu as pltpu
from jax.sharding import Mesh
from jax.sharding import PartitionSpec as P

clip_low = 0.8
clip_high = 1.25

bf16 = jnp.bfloat16
f32 = jnp.float32

NN = (((1,), (0,)), ((), ()))
NT = (((1,), (1,)), ((), ()))
TN = (((0,), (0,)), ((), ()))

QUAD = 4
SLOTS = 2
TILE = 8
LANE = 128


def mm(a, b, dims):
    return lax.dot_general(a, b, dims, preferred_element_type=f32)


def call(body, outs, flops, nbytes, **more):
    return pl.pallas_call(
        body,
        out_shape=outs,
        cost_estimate=pl.CostEstimate(flops=flops, bytes_accessed=nbytes, transcendentals=0),
        compiler_params=pltpu.CompilerParams(vmem_limit_bytes=24 * 1024 * 1024),
        **more,
    )


def me():
    return lax.axis_index("xh") * 2 + lax.axis_index("core")


def pieces(x):
    first = x.astype(bf16)
    rest = x - first.astype(f32)
    second = rest.astype(bf16)
    third = (rest - second.astype(f32)).astype(bf16)
    return jnp.concatenate([first, second, third], axis=0)


def pack_kernel(
    tokens_ref, cot_ref, probs_ref, ids_ref, seq_ref, ratios_ref, send_ref, table_ref, rows_ref
):
    count, width = tokens_ref.shape
    routes = ids_ref.shape[0]
    peers = send_ref.shape[0] // TILE
    experts = peers // QUAD
    down = lax.broadcasted_iota(jnp.int32, (count, count), 0)
    across = lax.broadcasted_iota(jnp.int32, (count, count), 1)

    def column(row):
        return jnp.sum(jnp.where(down == across, row, 0.0), axis=1, keepdims=True)

    labels = lax.broadcasted_iota(jnp.int32, (count, ratios_ref.shape[1]), 1).astype(f32)
    same = labels == column(seq_ref[...].astype(f32))
    picked = jnp.sum(jnp.where(same, ratios_ref[...], 0.0), axis=1, keepdims=True)
    weights = jnp.clip(picked, clip_low, clip_high)
    ids = ids_ref[...].astype(f32)
    peer = lax.broadcasted_iota(jnp.int32, (count, peers), 1)
    owner = lax.rem(peer, experts).astype(f32)
    first_slot = (lax.div(peer, experts) * SLOTS).astype(f32)
    member = jnp.zeros((count, peers), f32)
    prob_at = jnp.zeros((count, peers), f32)
    for k in range(routes):
        named = column(ids[k : k + 1, :]) == owner
        member = jnp.where(named, 1.0, member)
        prob_at = jnp.where(named, column(probs_ref[k : k + 1, :]), prob_at)
    scale_at = prob_at * weights
    lower = jnp.where(down > across, 1.0, 0.0).astype(bf16)
    before = mm(lower, member.astype(bf16), NN)
    cot = cot_ref[...]
    cots = jnp.concatenate([cot, cot, cot], axis=0)
    for s in range(SLOTS):
        here = (member > 0.0) & (before == first_slot + s)
        table = jnp.where(here, 1.0, 0.0).astype(bf16)
        table_ref[s, 0 : 3 * count, :] = pieces(jnp.where(here, prob_at, 0.0))
        table_ref[s, 3 * count : 4 * count, :] = table
        inputs = mm(table, tokens_ref[...], TN)
        seeds = mm(pieces(jnp.where(here, scale_at, 0.0)), cots, TN)
        for c in range(2):
            at = slice(c * LANE, (c + 1) * LANE)
            rows_ref[pl.ds(s * 4 + c, peers, stride=TILE), :] = inputs[:, at]
            rows_ref[pl.ds(s * 4 + 2 + c, peers, stride=TILE), :] = seeds[:, at]
    send_ref[...] = rows_ref[...].astype(bf16)


def gather_kernel(gate_ref, up_ref, down_ref, out_ref):
    width = gate_ref.shape[0]
    out_ref[0:width, :] = gate_ref[...]
    out_ref[width : 2 * width, :] = up_ref[...]
    out_ref[2 * width : 3 * width, :] = down_ref[...].T


def partial_kernel(came_ref, w0, w1, w2, w3, x_ref, out_ref, rows_ref, stage_ref):
    peers = came_ref.shape[0] // TILE
    blocks = peers // QUAD
    hidden = w0.shape[1]
    width = w0.shape[0] // 3
    wide = QUAD * width
    rows_ref[...] = came_ref[...].astype(f32)
    for j in range(TILE):
        stage_ref[j] = rows_ref[pl.ds(j, peers, stride=TILE), :].astype(bf16)
    mine = me()
    for k in range(QUAD):
        at = pl.ds(pl.multiple_of((mine ^ k) * blocks, blocks), blocks)
        for s in range(SLOTS):
            for c in range(4):
                column = (c // 2) * wide + k * width + (c % 2) * LANE
                x_ref[s * blocks : (s + 1) * blocks, column : column + LANE] = stage_ref[
                    s * 4 + c, at, :
                ]
    for part in range(3):
        total = jnp.zeros((SLOTS * blocks, hidden), f32)
        for k, w in enumerate((w0, w1, w2, w3)):
            column = (part // 2) * wide + k * width
            total = total + mm(
                x_ref[:, column : column + width], w[part * width : (part + 1) * width, :], NN
            )
        out_ref[:, part * hidden : (part + 1) * hidden] = total.astype(bf16)


def middle_kernel(parts_ref, out_ref):
    groups, rows, wide = parts_ref.shape
    hidden = wide // 3
    total = parts_ref[0].astype(f32)
    for g in range(1, groups):
        total = total + parts_ref[g].astype(f32)
    gate_sum = total[:, 0:hidden]
    up_sum = total[:, hidden : 2 * hidden]
    hidden_cot = total[:, 2 * hidden : 3 * hidden]
    sigmoid = 1.0 / (1.0 + jnp.exp(-gate_sum))
    active = gate_sum * sigmoid
    slopes = sigmoid * (1.0 + gate_sum * (1.0 - sigmoid))
    inner = (active * up_sum).astype(bf16)
    gate_cot = (hidden_cot * up_sum * slopes).astype(bf16)
    up_cot = (hidden_cot * active).astype(bf16)
    for g in range(groups):
        out_ref[g, :, 0:hidden] = inner
        out_ref[g, :, hidden : 2 * hidden] = gate_cot
        out_ref[g, :, 2 * hidden : 3 * hidden] = up_cot


def back_kernel(hgu_ref, w0, w1, w2, w3, send_ref, stage_ref, rows_ref):
    hidden = w0.shape[1]
    width = w0.shape[0] // 3
    blocks = hgu_ref.shape[0] // SLOTS
    peers = QUAD * blocks
    mine = me()
    inner = hgu_ref[:, 0:hidden]
    gate_cot = hgu_ref[:, hidden : 2 * hidden]
    up_cot = hgu_ref[:, 2 * hidden : 3 * hidden]
    for k, w in enumerate((w0, w1, w2, w3)):
        out = mm(inner, w[2 * width : 3 * width, :], NT)
        back = mm(gate_cot, w[0:width, :], NT) + mm(up_cot, w[width : 2 * width, :], NT)
        at = pl.ds(pl.multiple_of((mine ^ k) * blocks, blocks), blocks)
        for s in range(SLOTS):
            rows = slice(s * blocks, (s + 1) * blocks)
            for c in range(2):
                lanes = slice(c * LANE, (c + 1) * LANE)
                stage_ref[s * 4 + c, at, :] = out[rows, lanes]
                stage_ref[s * 4 + 2 + c, at, :] = back[rows, lanes]
    for j in range(TILE):
        rows_ref[pl.ds(j, peers, stride=TILE), :] = stage_ref[j]
    send_ref[...] = rows_ref[...].astype(bf16)


def grads_kernel(x_ref, hgu_ref, keep_ref, send_ref):
    hidden = hgu_ref.shape[1] // 3
    width = keep_ref.shape[1] // 3
    wide = QUAD * width
    for k in range(QUAD):
        out_ref = send_ref if k % 2 else keep_ref
        for part, (column, factor) in enumerate(((0, 1), (0, 2), (1, 0))):
            start = column * wide + k * width
            out_ref[k // 2, part * width : (part + 1) * width, :] = mm(
                x_ref[:, start : start + width],
                hgu_ref[:, factor * hidden : (factor + 1) * hidden],
                TN,
            ).astype(bf16)


def first_sum_kernel(keep_ref, came_ref, own_ref, other_ref):
    own_ref[...] = (keep_ref[0].astype(f32) + came_ref[0].astype(f32)).astype(bf16)
    other_ref[...] = (keep_ref[1].astype(f32) + came_ref[1].astype(f32)).astype(bf16)


def last_sum_kernel(own_ref, came_ref, gate_ref, up_ref, down_ref):
    width = gate_ref.shape[0]

    def total(part):
        at = slice(part * width, (part + 1) * width)
        return (own_ref[at, :].astype(f32) + came_ref[at, :].astype(f32)).astype(bf16)

    gate_ref[...] = total(0)
    up_ref[...] = total(1)
    down_ref[...] = total(2).T


def combine_kernel(table_ref, came_ref, out_ref, grad_ref, rows_ref):
    count, width = out_ref.shape
    peers = came_ref.shape[0] // TILE
    rows_ref[...] = came_ref[...].astype(f32)

    def picked(s, c):
        return jnp.concatenate(
            [rows_ref[pl.ds(s * 4 + c + i, peers, stride=TILE), :] for i in range(2)], axis=1
        ).astype(bf16)

    parts = jnp.zeros((3 * count, width), f32)
    grad = jnp.zeros((count, width), f32)
    for s in range(SLOTS):
        parts = parts + mm(table_ref[s, 0 : 3 * count, :], picked(s, 0), NN)
        grad = grad + mm(table_ref[s, 3 * count : 4 * count, :], picked(s, 2), NN)
    out_ref[...] = (
        parts[0:count] + parts[count : 2 * count] + parts[2 * count : 3 * count]
    ).astype(bf16)
    grad_ref[...] = grad.astype(bf16)


def local(
    tokens, cotangent, route_probs, expert_ids, seq_ids, ratios, gate_weight, up_weight, down_weight
):
    count, width = tokens.shape
    hidden = gate_weight.shape[2]
    sources = lax.axis_size("replica")
    groups = lax.axis_size("y")
    peers = QUAD * sources
    rows = SLOTS * sources
    shape = jax.ShapeDtypeStruct
    message = shape((peers * TILE, LANE), bf16)
    everyone = ("xh", "core", "replica")
    flip = [(0, 1), (1, 0)]
    product = 2 * rows * QUAD * width * hidden
    weight_bytes = 2 * 3 * QUAD * width * hidden

    def spread(x, axis):
        return lax.all_to_all(x, axis, split_axis=0, concat_axis=0, tiled=True)

    def messages(x):
        return spread(x.reshape(peers, TILE, LANE), everyone).reshape(peers * TILE, LANE)

    send, table = call(
        pack_kernel,
        (message, shape((SLOTS, 4 * count, peers), bf16)),
        16 * peers * count * width,
        4 * peers * TILE * LANE,
        scratch_shapes=[pltpu.VMEM((peers * TILE, LANE), f32)],
    )(
        tokens,
        cotangent,
        route_probs.T,
        expert_ids.T,
        seq_ids.reshape(1, count),
        ratios.reshape(1, -1),
    )
    came = messages(send)

    w0 = call(gather_kernel, shape((3 * width, hidden), bf16), 0, 12 * width * hidden)(
        gate_weight[0], up_weight[0], down_weight[0]
    )
    w2 = lax.ppermute(w0, "xh", flip)
    w1 = lax.ppermute(w0, "core", flip)
    w3 = lax.ppermute(w2, "core", flip)

    x, partial = call(
        partial_kernel,
        (shape((rows, 2 * QUAD * width), bf16), shape((rows, 3 * hidden), bf16)),
        3 * product,
        weight_bytes,
        scratch_shapes=[
            pltpu.VMEM((peers * TILE, LANE), f32),
            pltpu.VMEM((TILE, peers, LANE), bf16),
        ],
    )(came, w0, w1, w2, w3)
    parts = spread(partial.reshape(groups, rows // groups, 3 * hidden), "y")
    copies = call(
        middle_kernel,
        shape((groups, rows // groups, 3 * hidden), bf16),
        20 * rows * 3 * hidden,
        4 * rows * 3 * hidden,
    )(parts)
    hgu = spread(copies, "y").reshape(rows, 3 * hidden)
    sent_back = call(
        back_kernel,
        message,
        3 * product,
        weight_bytes,
        scratch_shapes=[
            pltpu.VMEM((TILE, peers, LANE), f32),
            pltpu.VMEM((peers * TILE, LANE), f32),
        ],
    )(hgu, w0, w1, w2, w3)

    pair = shape((2, 3 * width, hidden), bf16)
    one = shape((3 * width, hidden), bf16)
    x, hgu, sent_back = lax.optimization_barrier((x, hgu, sent_back))
    returned = messages(sent_back)
    keep, give = call(grads_kernel, (pair, pair), 3 * product, weight_bytes)(x, hgu)
    got = lax.ppermute(give, "core", flip)
    own, other = call(first_sum_kernel, (one, one), 6 * width * hidden, 2 * weight_bytes)(keep, got)
    theirs = lax.ppermute(other, "xh", flip)
    grads = call(
        last_sum_kernel,
        (
            shape((width, hidden), bf16),
            shape((width, hidden), bf16),
            shape((hidden, width), bf16),
        ),
        3 * width * hidden,
        weight_bytes,
    )(own, theirs)
    layer_out, grad_tokens = call(
        combine_kernel,
        (shape((count, width), bf16), shape((count, width), bf16)),
        16000 * peers * count * width,
        4 * peers * TILE * LANE,
        scratch_shapes=[pltpu.VMEM((peers * TILE, LANE), f32)],
    )(table, returned)
    return (layer_out, grad_tokens) + tuple(g[None] for g in grads)


def solution(mesh):
    groups = mesh.shape["expert"] // QUAD
    quads = Mesh(
        mesh.devices.reshape(groups, 2, 2, mesh.shape["replica"]), ("y", "xh", "core", "replica")
    )
    expert = ("y", "xh", "core")
    return jax.shard_map(
        local,
        mesh=quads,
        in_specs=(
            P("replica", expert),
            P("replica", expert),
            P("replica", None),
            P("replica", None),
            P("replica"),
            P(),
            P("replica", expert, None),
            P("replica", expert, None),
            P("replica", None, expert),
        ),
        out_specs=(
            P("replica", expert),
            P("replica", expert),
            P("replica", expert, None),
            P("replica", expert, None),
            P("replica", None, expert),
        ),
        check_vma=False,
    )
```

```python
import jax
import jax.numpy as jnp
from jax import lax
from jax.experimental import pallas as pl
from jax.experimental.pallas import tpu as pltpu
from jax.sharding import Mesh
from jax.sharding import PartitionSpec as P

clip_low = 0.8
clip_high = 1.25

bf16 = jnp.bfloat16
f32 = jnp.float32

NN = (((1,), (0,)), ((), ()))
NT = (((1,), (1,)), ((), ()))
TN = (((0,), (0,)), ((), ()))

QUAD = 4
SLOTS = 2
TILE = 8
LANE = 128


def mm(a, b, dims):
    return lax.dot_general(a, b, dims, preferred_element_type=f32)


def call(body, outs, flops, nbytes, room=24, **more):
    return pl.pallas_call(
        body,
        out_shape=outs,
        cost_estimate=pl.CostEstimate(flops=flops, bytes_accessed=nbytes, transcendentals=0),
        compiler_params=pltpu.CompilerParams(vmem_limit_bytes=room * 1024 * 1024),
        **more,
    )


def me():
    return lax.axis_index("yl") * 2 + lax.axis_index("core")


def pieces(x):
    first = x.astype(bf16)
    rest = x - first.astype(f32)
    second = rest.astype(bf16)
    third = (rest - second.astype(f32)).astype(bf16)
    return jnp.concatenate([first, second, third], axis=0)


def pack_kernel(*refs):
    arrays, (send_ref, table_ref, rows_ref), held, sem = refs[:6], refs[6:9], refs[9:15], refs[15]
    copies = [pltpu.make_async_copy(a, b, sem.at[i]) for i, (a, b) in enumerate(zip(arrays, held))]
    for copy in copies:
        copy.start()
    for copy in copies:
        copy.wait()
    tokens_ref, cot_ref, probs_ref, ids_ref, seq_ref, ratios_ref = held
    count, width = tokens_ref.shape
    routes = ids_ref.shape[0]
    peers = send_ref.shape[0] // TILE
    experts = peers // QUAD
    down = lax.broadcasted_iota(jnp.int32, (count, count), 0)
    across = lax.broadcasted_iota(jnp.int32, (count, count), 1)

    def column(row):
        return jnp.sum(jnp.where(down == across, row, 0.0), axis=1, keepdims=True)

    labels = lax.broadcasted_iota(jnp.int32, (count, ratios_ref.shape[1]), 1).astype(f32)
    same = labels == column(seq_ref[...].astype(f32))
    picked = jnp.sum(jnp.where(same, ratios_ref[...], 0.0), axis=1, keepdims=True)
    weights = jnp.clip(picked, clip_low, clip_high)
    ids = ids_ref[...].astype(f32)
    peer = lax.broadcasted_iota(jnp.int32, (count, peers), 1)
    owner = lax.rem(peer, experts).astype(f32)
    first_slot = (lax.div(peer, experts) * SLOTS).astype(f32)
    member = jnp.zeros((count, peers), f32)
    prob_at = jnp.zeros((count, peers), f32)
    for k in range(routes):
        named = column(ids[k : k + 1, :]) == owner
        member = jnp.where(named, 1.0, member)
        prob_at = jnp.where(named, column(probs_ref[k : k + 1, :]), prob_at)
    scale_at = prob_at * weights
    lower = jnp.where(down > across, 1.0, 0.0).astype(bf16)
    before = mm(lower, member.astype(bf16), NN)
    cot = cot_ref[...]
    cots = jnp.concatenate([cot, cot, cot], axis=0)
    for s in range(SLOTS):
        here = (member > 0.0) & (before == first_slot + s)
        table = jnp.where(here, 1.0, 0.0).astype(bf16)
        table_ref[s, 0 : 3 * count, :] = pieces(jnp.where(here, prob_at, 0.0))
        table_ref[s, 3 * count : 4 * count, :] = table
        inputs = mm(table, tokens_ref[...], TN)
        seeds = mm(pieces(jnp.where(here, scale_at, 0.0)), cots, TN)
        for c in range(2):
            at = slice(c * LANE, (c + 1) * LANE)
            rows_ref[pl.ds(s * 4 + c, peers, stride=TILE), :] = inputs[:, at]
            rows_ref[pl.ds(s * 4 + 2 + c, peers, stride=TILE), :] = seeds[:, at]
    send_ref[...] = rows_ref[...].astype(bf16)


def gather_kernel(gate_ref, up_ref, down_ref, out_ref):
    width = gate_ref.shape[0]
    out_ref[0:width, :] = gate_ref[...]
    out_ref[width : 2 * width, :] = up_ref[...]
    out_ref[2 * width : 3 * width, :] = down_ref[...].T


def partial_kernel(came_ref, w0, w1, w2, w3, x_ref, out_ref, rows_ref, stage_ref):
    peers = came_ref.shape[0] // TILE
    blocks = peers // QUAD
    hidden = w0.shape[1]
    width = w0.shape[0] // 3
    wide = QUAD * width
    rows_ref[...] = came_ref[...].astype(f32)
    for j in range(TILE):
        stage_ref[j] = rows_ref[pl.ds(j, peers, stride=TILE), :].astype(bf16)
    mine = me()
    for k in range(QUAD):
        at = pl.ds(pl.multiple_of((mine ^ k) * blocks, blocks), blocks)
        for s in range(SLOTS):
            for c in range(4):
                column = (c // 2) * wide + k * width + (c % 2) * LANE
                x_ref[s * blocks : (s + 1) * blocks, column : column + LANE] = stage_ref[
                    s * 4 + c, at, :
                ]
    for part in range(3):
        total = jnp.zeros((SLOTS * blocks, hidden), f32)
        for k, w in enumerate((w0, w1, w2, w3)):
            column = (part // 2) * wide + k * width
            total = total + mm(
                x_ref[:, column : column + width], w[part * width : (part + 1) * width, :], NN
            )
        out_ref[:, part * hidden : (part + 1) * hidden] = total.astype(bf16)


def middle_kernel(parts_ref, out_ref):
    groups, rows, wide = parts_ref.shape
    hidden = wide // 3
    total = parts_ref[0].astype(f32)
    for g in range(1, groups):
        total = total + parts_ref[g].astype(f32)
    gate_sum = total[:, 0:hidden]
    up_sum = total[:, hidden : 2 * hidden]
    hidden_cot = total[:, 2 * hidden : 3 * hidden]
    sigmoid = 1.0 / (1.0 + jnp.exp(-gate_sum))
    active = gate_sum * sigmoid
    slopes = sigmoid * (1.0 + gate_sum * (1.0 - sigmoid))
    inner = (active * up_sum).astype(bf16)
    gate_cot = (hidden_cot * up_sum * slopes).astype(bf16)
    up_cot = (hidden_cot * active).astype(bf16)
    for g in range(groups):
        out_ref[g, :, 0:hidden] = inner
        out_ref[g, :, hidden : 2 * hidden] = gate_cot
        out_ref[g, :, 2 * hidden : 3 * hidden] = up_cot


def back_kernel(hgu_ref, w0, w1, w2, w3, send_ref, stage_ref, rows_ref):
    hidden = w0.shape[1]
    width = w0.shape[0] // 3
    blocks = hgu_ref.shape[0] // SLOTS
    peers = QUAD * blocks
    mine = me()
    inner = hgu_ref[:, 0:hidden]
    gate_cot = hgu_ref[:, hidden : 2 * hidden]
    up_cot = hgu_ref[:, 2 * hidden : 3 * hidden]
    for k, w in enumerate((w0, w1, w2, w3)):
        out = mm(inner, w[2 * width : 3 * width, :], NT)
        back = mm(gate_cot, w[0:width, :], NT) + mm(up_cot, w[width : 2 * width, :], NT)
        at = pl.ds(pl.multiple_of((mine ^ k) * blocks, blocks), blocks)
        for s in range(SLOTS):
            rows = slice(s * blocks, (s + 1) * blocks)
            for c in range(2):
                lanes = slice(c * LANE, (c + 1) * LANE)
                stage_ref[s * 4 + c, at, :] = out[rows, lanes]
                stage_ref[s * 4 + 2 + c, at, :] = back[rows, lanes]
    for j in range(TILE):
        rows_ref[pl.ds(j, peers, stride=TILE), :] = stage_ref[j]
    send_ref[...] = rows_ref[...].astype(bf16)


def grads_kernel(x_ref, hgu_ref, keep_ref, send_ref):
    hidden = hgu_ref.shape[1] // 3
    width = keep_ref.shape[1] // 3
    wide = QUAD * width
    for k in range(QUAD):
        out_ref = send_ref if k % 2 else keep_ref
        for part, (column, factor) in enumerate(((0, 1), (0, 2), (1, 0))):
            start = column * wide + k * width
            out_ref[k // 2, part * width : (part + 1) * width, :] = mm(
                x_ref[:, start : start + width],
                hgu_ref[:, factor * hidden : (factor + 1) * hidden],
                TN,
            ).astype(bf16)


def first_sum_kernel(keep_ref, came_ref, own_ref, other_ref):
    own_ref[...] = (keep_ref[0].astype(f32) + came_ref[0].astype(f32)).astype(bf16)
    other_ref[...] = (keep_ref[1].astype(f32) + came_ref[1].astype(f32)).astype(bf16)


def last_sum_kernel(own_ref, came_ref, gate_ref, up_ref, down_ref):
    width = gate_ref.shape[0]

    def total(part):
        at = slice(part * width, (part + 1) * width)
        return (own_ref[at, :].astype(f32) + came_ref[at, :].astype(f32)).astype(bf16)

    gate_ref[...] = total(0)
    up_ref[...] = total(1)
    down_ref[...] = total(2).T


def combine_kernel(table_ref, came_ref, out_ref, grad_ref, rows_ref):
    count, width = out_ref.shape
    peers = came_ref.shape[0] // TILE
    rows_ref[...] = came_ref[...].astype(f32)

    def picked(s, c):
        return jnp.concatenate(
            [rows_ref[pl.ds(s * 4 + c + i, peers, stride=TILE), :] for i in range(2)], axis=1
        ).astype(bf16)

    parts = jnp.zeros((3 * count, width), f32)
    grad = jnp.zeros((count, width), f32)
    for s in range(SLOTS):
        parts = parts + mm(table_ref[s, 0 : 3 * count, :], picked(s, 0), NN)
        grad = grad + mm(table_ref[s, 3 * count : 4 * count, :], picked(s, 2), NN)
    out_ref[...] = (
        parts[0:count] + parts[count : 2 * count] + parts[2 * count : 3 * count]
    ).astype(bf16)
    grad_ref[...] = grad.astype(bf16)


def local(
    tokens, cotangent, route_probs, expert_ids, seq_ids, ratios, gate_weight, up_weight, down_weight
):
    count, width = tokens.shape
    hidden = gate_weight.shape[2]
    sources = lax.axis_size("replica")
    others = ("xh", "yh")
    groups = lax.axis_size("xh") * lax.axis_size("yh")
    peers = QUAD * sources
    rows = SLOTS * sources
    shape = jax.ShapeDtypeStruct
    message = shape((peers * TILE, LANE), bf16)
    everyone = ("yl", "core", "replica")
    flip = [(0, 1), (1, 0)]
    product = 2 * rows * QUAD * width * hidden
    weight_bytes = 2 * 3 * QUAD * width * hidden

    def spread(x, axis):
        return lax.all_to_all(x, axis, split_axis=0, concat_axis=0, tiled=True)

    def messages(x):
        return spread(x.reshape(peers, TILE, LANE), everyone).reshape(peers * TILE, LANE)

    arrays = (
        tokens,
        cotangent,
        route_probs.T,
        expert_ids.T,
        seq_ids.reshape(1, count),
        ratios.reshape(1, -1),
    )
    send, table = call(
        pack_kernel,
        (message, shape((SLOTS, 4 * count, peers), bf16)),
        16 * peers * count * width,
        4 * peers * TILE * LANE,
        60,
        in_specs=[pl.BlockSpec(memory_space=pl.ANY)] * len(arrays),
        scratch_shapes=[pltpu.VMEM((peers * TILE, LANE), f32)]
        + [pltpu.VMEM(a.shape, a.dtype) for a in arrays]
        + [pltpu.SemaphoreType.DMA((len(arrays),))],
    )(*arrays)
    came = messages(send)

    w0 = call(gather_kernel, shape((3 * width, hidden), bf16), 0, 12 * width * hidden)(
        gate_weight[0], up_weight[0], down_weight[0]
    )
    w2 = lax.ppermute(w0, "yl", flip)
    w1 = lax.ppermute(w0, "core", flip)
    w3 = lax.ppermute(w2, "core", flip)

    x, partial = call(
        partial_kernel,
        (shape((rows, 2 * QUAD * width), bf16), shape((rows, 3 * hidden), bf16)),
        3 * product,
        weight_bytes,
        scratch_shapes=[
            pltpu.VMEM((peers * TILE, LANE), f32),
            pltpu.VMEM((TILE, peers, LANE), bf16),
        ],
    )(came, w0, w1, w2, w3)
    parts = spread(partial.reshape(groups, rows // groups, 3 * hidden), others)
    copies = call(
        middle_kernel,
        shape((groups, rows // groups, 3 * hidden), bf16),
        20 * rows * 3 * hidden,
        4 * rows * 3 * hidden,
    )(parts)
    hgu = spread(copies, others).reshape(rows, 3 * hidden)
    sent_back = call(
        back_kernel,
        message,
        3 * product,
        weight_bytes,
        scratch_shapes=[
            pltpu.VMEM((TILE, peers, LANE), f32),
            pltpu.VMEM((peers * TILE, LANE), f32),
        ],
    )(hgu, w0, w1, w2, w3)

    pair = shape((2, 3 * width, hidden), bf16)
    one = shape((3 * width, hidden), bf16)
    returned = messages(sent_back)
    keep, give = call(grads_kernel, (pair, pair), 3 * product, weight_bytes)(x, hgu)
    got = lax.ppermute(give, "core", flip)
    own, other = call(first_sum_kernel, (one, one), 6 * width * hidden, 2 * weight_bytes)(keep, got)
    theirs = lax.ppermute(other, "yl", flip)
    grads = call(
        last_sum_kernel,
        (
            shape((width, hidden), bf16),
            shape((width, hidden), bf16),
            shape((hidden, width), bf16),
        ),
        3 * width * hidden,
        weight_bytes,
    )(own, theirs)
    layer_out, grad_tokens = call(
        combine_kernel,
        (shape((count, width), bf16), shape((count, width), bf16)),
        16000 * peers * count * width,
        4 * peers * TILE * LANE,
        scratch_shapes=[pltpu.VMEM((peers * TILE, LANE), f32)],
    )(table, returned)
    return (layer_out, grad_tokens) + tuple(g[None] for g in grads)


def solution(mesh):
    axes = ("yh", "yl", "xh", "core")
    shape = (mesh.shape["expert"] // 8, 2, 2, 2, mesh.shape["replica"])
    quads = Mesh(mesh.devices.reshape(shape), axes + ("replica",))
    expert = axes
    return jax.shard_map(
        local,
        mesh=quads,
        in_specs=(
            P("replica", expert),
            P("replica", expert),
            P("replica", None),
            P("replica", None),
            P("replica"),
            P(),
            P("replica", expert, None),
            P("replica", expert, None),
            P("replica", None, expert),
        ),
        out_specs=(
            P("replica", expert),
            P("replica", expert),
            P("replica", expert, None),
            P("replica", expert, None),
            P("replica", None, expert),
        ),
        check_vma=False,
    )
```

```python
import jax
import jax.numpy as jnp
from jax import lax
from jax.experimental import pallas as pl
from jax.experimental.pallas import tpu as pltpu
from jax.sharding import Mesh
from jax.sharding import PartitionSpec as P

clip_low = 0.8
clip_high = 1.25

bf16 = jnp.bfloat16
f32 = jnp.float32

NN = (((1,), (0,)), ((), ()))
NT = (((1,), (1,)), ((), ()))
TN = (((0,), (0,)), ((), ()))

QUAD = 4
SLOTS = 2
TILE = 8
LANE = 128
ROOM = 50
LARGE = 60


def mm(a, b, dims):
    return lax.dot_general(a, b, dims, preferred_element_type=f32)


def call(body, outs, flops, nbytes, room=24, **more):
    return pl.pallas_call(
        body,
        out_shape=outs,
        cost_estimate=pl.CostEstimate(flops=flops, bytes_accessed=nbytes, transcendentals=0),
        compiler_params=pltpu.CompilerParams(vmem_limit_bytes=room * 1024 * 1024),
        **more,
    )


def me():
    return lax.axis_index("yl") * 2 + lax.axis_index("core")


def pieces(x):
    first = x.astype(bf16)
    rest = x - first.astype(f32)
    second = rest.astype(bf16)
    third = (rest - second.astype(f32)).astype(bf16)
    return jnp.concatenate([first, second, third], axis=0)


def pack_kernel(*refs):
    arrays, (send_ref, table_ref, rows_ref), held, sem = refs[:6], refs[6:9], refs[9:15], refs[15]
    copies = [pltpu.make_async_copy(a, b, sem.at[i]) for i, (a, b) in enumerate(zip(arrays, held))]
    for copy in copies:
        copy.start()
    for copy in copies:
        copy.wait()
    tokens_ref, cot_ref, probs_ref, ids_ref, seq_ref, ratios_ref = held
    count, width = tokens_ref.shape
    routes = ids_ref.shape[0]
    peers = send_ref.shape[0] // TILE
    experts = peers // QUAD
    down = lax.broadcasted_iota(jnp.int32, (count, count), 0)
    across = lax.broadcasted_iota(jnp.int32, (count, count), 1)

    def column(row):
        return jnp.sum(jnp.where(down == across, row, 0.0), axis=1, keepdims=True)

    labels = lax.broadcasted_iota(jnp.int32, (count, ratios_ref.shape[1]), 1).astype(f32)
    same = labels == column(seq_ref[...].astype(f32))
    picked = jnp.sum(jnp.where(same, ratios_ref[...], 0.0), axis=1, keepdims=True)
    weights = jnp.clip(picked, clip_low, clip_high)
    ids = ids_ref[...].astype(f32)
    peer = lax.broadcasted_iota(jnp.int32, (count, peers), 1)
    owner = lax.rem(peer, experts).astype(f32)
    first_slot = (lax.div(peer, experts) * SLOTS).astype(f32)
    member = jnp.zeros((count, peers), f32)
    prob_at = jnp.zeros((count, peers), f32)
    for k in range(routes):
        named = column(ids[k : k + 1, :]) == owner
        member = jnp.where(named, 1.0, member)
        prob_at = jnp.where(named, column(probs_ref[k : k + 1, :]), prob_at)
    scale_at = prob_at * weights
    lower = jnp.where(down > across, 1.0, 0.0).astype(bf16)
    before = mm(lower, member.astype(bf16), NN)
    cot = cot_ref[...]
    cots = jnp.concatenate([cot, cot, cot], axis=0)
    for s in range(SLOTS):
        here = (member > 0.0) & (before == first_slot + s)
        table = jnp.where(here, 1.0, 0.0).astype(bf16)
        table_ref[s, 0 : 3 * count, :] = pieces(jnp.where(here, prob_at, 0.0))
        table_ref[s, 3 * count : 4 * count, :] = table
        inputs = mm(table, tokens_ref[...], TN)
        seeds = mm(pieces(jnp.where(here, scale_at, 0.0)), cots, TN)
        for c in range(2):
            at = slice(c * LANE, (c + 1) * LANE)
            rows_ref[pl.ds(s * 4 + c, peers, stride=TILE), :] = inputs[:, at]
            rows_ref[pl.ds(s * 4 + 2 + c, peers, stride=TILE), :] = seeds[:, at]
    send_ref[...] = rows_ref[...].astype(bf16)


def gather_kernel(gate_ref, up_ref, down_ref, out_ref):
    width = gate_ref.shape[0]
    out_ref[0:width, :] = gate_ref[...]
    out_ref[width : 2 * width, :] = up_ref[...]
    out_ref[2 * width : 3 * width, :] = down_ref[...].T


def partial_kernel(came_ref, w0, w1, w2, w3, x_ref, out_ref, rows_ref, stage_ref, held, sem):
    peers = came_ref.shape[0] // TILE
    blocks = peers // QUAD
    hidden = w0.shape[1]
    width = w0.shape[0] // 3
    fetches = []
    for part in range(3):
        for k, w in enumerate((w0, w1, w2, w3)):
            at = pl.ds(part * width, width)
            fetches.append(
                pltpu.make_async_copy(w.at[at, :], held.at[k, at, :], sem.at[QUAD * part + k])
            )
            fetches[-1].start()
    wide = QUAD * width
    rows_ref[...] = came_ref[...].astype(f32)
    for j in range(TILE):
        stage_ref[j] = rows_ref[pl.ds(j, peers, stride=TILE), :].astype(bf16)
    mine = me()
    for k in range(QUAD):
        at = pl.ds(pl.multiple_of((mine ^ k) * blocks, blocks), blocks)
        for s in range(SLOTS):
            for c in range(4):
                column = (c // 2) * wide + k * width + (c % 2) * LANE
                x_ref[s * blocks : (s + 1) * blocks, column : column + LANE] = stage_ref[
                    s * 4 + c, at, :
                ]
    for part in range(3):
        total = jnp.zeros((SLOTS * blocks, hidden), f32)
        for k in range(QUAD):
            column = (part // 2) * wide + k * width
            fetches[QUAD * part + k].wait()
            total = total + mm(
                x_ref[:, column : column + width],
                held[k, part * width : (part + 1) * width, :],
                NN,
            )
        out_ref[:, part * hidden : (part + 1) * hidden] = total.astype(bf16)


def middle_kernel(parts_ref, out_ref):
    groups, rows, wide = parts_ref.shape
    hidden = wide // 3
    total = parts_ref[0].astype(f32)
    for g in range(1, groups):
        total = total + parts_ref[g].astype(f32)
    gate_sum = total[:, 0:hidden]
    up_sum = total[:, hidden : 2 * hidden]
    hidden_cot = total[:, 2 * hidden : 3 * hidden]
    sigmoid = 1.0 / (1.0 + jnp.exp(-gate_sum))
    active = gate_sum * sigmoid
    slopes = sigmoid * (1.0 + gate_sum * (1.0 - sigmoid))
    inner = (active * up_sum).astype(bf16)
    gate_cot = (hidden_cot * up_sum * slopes).astype(bf16)
    up_cot = (hidden_cot * active).astype(bf16)
    for g in range(groups):
        out_ref[g, :, 0:hidden] = inner
        out_ref[g, :, hidden : 2 * hidden] = gate_cot
        out_ref[g, :, 2 * hidden : 3 * hidden] = up_cot


def back_kernel(hgu_ref, w0, w1, w2, w3, send_ref, stage_ref, rows_ref, held, sem):
    fetches = []
    for k, w in enumerate((w0, w1, w2, w3)):
        fetches.append(pltpu.make_async_copy(w, held.at[k], sem.at[k]))
        fetches[-1].start()
    hidden = w0.shape[1]
    width = w0.shape[0] // 3
    blocks = hgu_ref.shape[0] // SLOTS
    peers = QUAD * blocks
    mine = me()
    inner = hgu_ref[:, 0:hidden]
    gate_cot = hgu_ref[:, hidden : 2 * hidden]
    up_cot = hgu_ref[:, 2 * hidden : 3 * hidden]
    for k in range(QUAD):
        fetches[k].wait()
        out = mm(inner, held[k, 2 * width : 3 * width, :], NT)
        back = mm(gate_cot, held[k, 0:width, :], NT) + mm(
            up_cot, held[k, width : 2 * width, :], NT
        )
        at = pl.ds(pl.multiple_of((mine ^ k) * blocks, blocks), blocks)
        for s in range(SLOTS):
            rows = slice(s * blocks, (s + 1) * blocks)
            for c in range(2):
                lanes = slice(c * LANE, (c + 1) * LANE)
                stage_ref[s * 4 + c, at, :] = out[rows, lanes]
                stage_ref[s * 4 + 2 + c, at, :] = back[rows, lanes]
    for j in range(TILE):
        rows_ref[pl.ds(j, peers, stride=TILE), :] = stage_ref[j]
    send_ref[...] = rows_ref[...].astype(bf16)


def grads_kernel(x_ref, hgu_ref, keep_ref, send_ref):
    hidden = hgu_ref.shape[1] // 3
    width = keep_ref.shape[1] // 3
    wide = QUAD * width
    for k in range(QUAD):
        out_ref = send_ref if k % 2 else keep_ref
        for part, (column, factor) in enumerate(((0, 1), (0, 2), (1, 0))):
            start = column * wide + k * width
            out_ref[k // 2, part * width : (part + 1) * width, :] = mm(
                x_ref[:, start : start + width],
                hgu_ref[:, factor * hidden : (factor + 1) * hidden],
                TN,
            ).astype(bf16)


def first_sum_kernel(keep_ref, came_ref, own_ref, other_ref):
    own_ref[...] = (keep_ref[0].astype(f32) + came_ref[0].astype(f32)).astype(bf16)
    other_ref[...] = (keep_ref[1].astype(f32) + came_ref[1].astype(f32)).astype(bf16)


def last_sum_kernel(own_ref, came_ref, gate_ref, up_ref, down_ref):
    width = gate_ref.shape[0]

    def total(part):
        at = slice(part * width, (part + 1) * width)
        return (own_ref[at, :].astype(f32) + came_ref[at, :].astype(f32)).astype(bf16)

    gate_ref[...] = total(0)
    up_ref[...] = total(1)
    down_ref[...] = total(2).T


def combine_kernel(table_ref, came_ref, out_ref, grad_ref, rows_ref):
    count, width = out_ref.shape
    peers = came_ref.shape[0] // TILE
    rows_ref[...] = came_ref[...].astype(f32)

    def picked(s, c):
        return jnp.concatenate(
            [rows_ref[pl.ds(s * 4 + c + i, peers, stride=TILE), :] for i in range(2)], axis=1
        ).astype(bf16)

    parts = jnp.zeros((3 * count, width), f32)
    grad = jnp.zeros((count, width), f32)
    for s in range(SLOTS):
        parts = parts + mm(table_ref[s, 0 : 3 * count, :], picked(s, 0), NN)
        grad = grad + mm(table_ref[s, 3 * count : 4 * count, :], picked(s, 2), NN)
    out_ref[...] = (
        parts[0:count] + parts[count : 2 * count] + parts[2 * count : 3 * count]
    ).astype(bf16)
    grad_ref[...] = grad.astype(bf16)


def local(
    tokens, cotangent, route_probs, expert_ids, seq_ids, ratios, gate_weight, up_weight, down_weight
):
    count, width = tokens.shape
    hidden = gate_weight.shape[2]
    sources = lax.axis_size("replica")
    others = ("xh", "yh")
    groups = lax.axis_size("xh") * lax.axis_size("yh")
    peers = QUAD * sources
    rows = SLOTS * sources
    shape = jax.ShapeDtypeStruct
    message = shape((peers * TILE, LANE), bf16)
    everyone = ("yl", "core", "replica")
    flip = [(0, 1), (1, 0)]
    product = 2 * rows * QUAD * width * hidden
    weight_bytes = 2 * 3 * QUAD * width * hidden

    def spread(x, axis):
        return lax.all_to_all(x, axis, split_axis=0, concat_axis=0, tiled=True)

    def messages(x):
        return spread(x.reshape(peers, TILE, LANE), everyone).reshape(peers * TILE, LANE)

    arrays = (
        tokens,
        cotangent,
        route_probs.T,
        expert_ids.T,
        seq_ids.reshape(1, count),
        ratios.reshape(1, -1),
    )
    send, table = call(
        pack_kernel,
        (message, shape((SLOTS, 4 * count, peers), bf16)),
        16 * peers * count * width,
        4 * peers * TILE * LANE,
        60,
        in_specs=[pl.BlockSpec(memory_space=pl.ANY)] * len(arrays),
        scratch_shapes=[pltpu.VMEM((peers * TILE, LANE), f32)]
        + [pltpu.VMEM(a.shape, a.dtype) for a in arrays]
        + [pltpu.SemaphoreType.DMA((len(arrays),))],
    )(*arrays)
    came = messages(send)

    w0 = call(gather_kernel, shape((3 * width, hidden), bf16), 0, 12 * width * hidden, ROOM)(
        gate_weight[0], up_weight[0], down_weight[0]
    )
    w2 = lax.ppermute(w0, "yl", flip)
    w1 = lax.ppermute(w0, "core", flip)
    w3 = lax.ppermute(w2, "core", flip)

    x, partial = call(
        partial_kernel,
        (shape((rows, 2 * QUAD * width), bf16), shape((rows, 3 * hidden), bf16)),
        3 * product,
        weight_bytes,
        ROOM,
        in_specs=[pl.BlockSpec(memory_space=pltpu.VMEM)]
        + [pl.BlockSpec(memory_space=pl.ANY)] * QUAD,
        scratch_shapes=[
            pltpu.VMEM((peers * TILE, LANE), f32),
            pltpu.VMEM((TILE, peers, LANE), bf16),
            pltpu.VMEM((QUAD, 3 * width, hidden), bf16),
            pltpu.SemaphoreType.DMA((3 * QUAD,)),
        ],
    )(came, w0, w1, w2, w3)
    parts = spread(partial.reshape(groups, rows // groups, 3 * hidden), others)
    copies = call(
        middle_kernel,
        shape((groups, rows // groups, 3 * hidden), bf16),
        20 * rows * 3 * hidden,
        4 * rows * 3 * hidden,
    )(parts)
    hgu = spread(copies, others).reshape(rows, 3 * hidden)
    sent_back = call(
        back_kernel,
        message,
        3 * product,
        weight_bytes,
        ROOM,
        in_specs=[pl.BlockSpec(memory_space=pltpu.VMEM)]
        + [pl.BlockSpec(memory_space=pl.ANY)] * QUAD,
        scratch_shapes=[
            pltpu.VMEM((TILE, peers, LANE), f32),
            pltpu.VMEM((peers * TILE, LANE), f32),
            pltpu.VMEM((QUAD, 3 * width, hidden), bf16),
            pltpu.SemaphoreType.DMA((QUAD,)),
        ],
    )(hgu, w0, w1, w2, w3)

    pair = shape((2, 3 * width, hidden), bf16)
    one = shape((3 * width, hidden), bf16)
    returned = messages(sent_back)
    keep, give = call(grads_kernel, (pair, pair), 3 * product, weight_bytes, LARGE)(x, hgu)
    got = lax.ppermute(give, "core", flip)
    own, other = call(
        first_sum_kernel, (one, one), 6 * width * hidden, 2 * weight_bytes, LARGE
    )(keep, got)
    theirs = lax.ppermute(other, "yl", flip)
    grads = call(
        last_sum_kernel,
        (
            shape((width, hidden), bf16),
            shape((width, hidden), bf16),
            shape((hidden, width), bf16),
        ),
        3 * width * hidden,
        weight_bytes,
    )(own, theirs)
    layer_out, grad_tokens = call(
        combine_kernel,
        (shape((count, width), bf16), shape((count, width), bf16)),
        16000 * peers * count * width,
        4 * peers * TILE * LANE,
        scratch_shapes=[pltpu.VMEM((peers * TILE, LANE), f32)],
    )(table, returned)
    return (layer_out, grad_tokens) + tuple(g[None] for g in grads)


def solution(mesh):
    axes = ("yh", "yl", "xh", "core")
    shape = (mesh.shape["expert"] // 8, 2, 2, 2, mesh.shape["replica"])
    quads = Mesh(mesh.devices.reshape(shape), axes + ("replica",))
    expert = axes
    return jax.shard_map(
        local,
        mesh=quads,
        in_specs=(
            P("replica", expert),
            P("replica", expert),
            P("replica", None),
            P("replica", None),
            P("replica"),
            P(),
            P("replica", expert, None),
            P("replica", expert, None),
            P("replica", None, expert),
        ),
        out_specs=(
            P("replica", expert),
            P("replica", expert),
            P("replica", expert, None),
            P("replica", expert, None),
            P("replica", None, expert),
        ),
        check_vma=False,
    )
```

```python
import jax
import jax.numpy as jnp
from jax import lax
from jax.experimental import pallas as pl
from jax.experimental.pallas import tpu as pltpu
from jax.sharding import Mesh
from jax.sharding import PartitionSpec as P

clip_low = 0.8
clip_high = 1.25

bf16 = jnp.bfloat16
f32 = jnp.float32

NN = (((1,), (0,)), ((), ()))
NT = (((1,), (1,)), ((), ()))
TN = (((0,), (0,)), ((), ()))

QUAD = 4
SLOTS = 2
TILE = 8
LANE = 128
ROOM = 50
LARGE = 60


def mm(a, b, dims):
    return lax.dot_general(a, b, dims, preferred_element_type=f32)


def call(body, outs, flops, nbytes, room=24, **more):
    return pl.pallas_call(
        body,
        out_shape=outs,
        cost_estimate=pl.CostEstimate(flops=flops, bytes_accessed=nbytes, transcendentals=0),
        compiler_params=pltpu.CompilerParams(vmem_limit_bytes=room * 1024 * 1024),
        **more,
    )


def me():
    return lax.axis_index("yl") * 2 + lax.axis_index("core")


def pieces(x):
    first = x.astype(bf16)
    rest = x - first.astype(f32)
    second = rest.astype(bf16)
    third = (rest - second.astype(f32)).astype(bf16)
    return jnp.concatenate([first, second, third], axis=0)


def pack_kernel(*refs):
    arrays, (send_ref, table_ref, rows_ref), held, sem = refs[:6], refs[6:9], refs[9:15], refs[15]
    copies = [pltpu.make_async_copy(a, b, sem.at[i]) for i, (a, b) in enumerate(zip(arrays, held))]
    for copy in copies:
        copy.start()
    for copy in copies:
        copy.wait()
    tokens_ref, cot_ref, probs_ref, ids_ref, seq_ref, ratios_ref = held
    count, width = tokens_ref.shape
    routes = ids_ref.shape[0]
    peers = send_ref.shape[0] // TILE
    experts = peers // QUAD
    down = lax.broadcasted_iota(jnp.int32, (count, count), 0)
    across = lax.broadcasted_iota(jnp.int32, (count, count), 1)

    def column(row):
        return jnp.sum(jnp.where(down == across, row, 0.0), axis=1, keepdims=True)

    labels = lax.broadcasted_iota(jnp.int32, (count, ratios_ref.shape[1]), 1).astype(f32)
    same = labels == column(seq_ref[...].astype(f32))
    picked = jnp.sum(jnp.where(same, ratios_ref[...], 0.0), axis=1, keepdims=True)
    weights = jnp.clip(picked, clip_low, clip_high)
    ids = ids_ref[...].astype(f32)
    peer = lax.broadcasted_iota(jnp.int32, (count, peers), 1)
    owner = lax.rem(peer, experts).astype(f32)
    first_slot = (lax.div(peer, experts) * SLOTS).astype(f32)
    member = jnp.zeros((count, peers), f32)
    prob_at = jnp.zeros((count, peers), f32)
    for k in range(routes):
        named = column(ids[k : k + 1, :]) == owner
        member = jnp.where(named, 1.0, member)
        prob_at = jnp.where(named, column(probs_ref[k : k + 1, :]), prob_at)
    scale_at = prob_at * weights
    lower = jnp.where(down > across, 1.0, 0.0).astype(bf16)
    before = mm(lower, member.astype(bf16), NN)
    cot = cot_ref[...]
    cots = jnp.concatenate([cot, cot, cot], axis=0)
    for s in range(SLOTS):
        here = (member > 0.0) & (before == first_slot + s)
        table = jnp.where(here, 1.0, 0.0).astype(bf16)
        table_ref[s, 0 : 3 * count, :] = pieces(jnp.where(here, prob_at, 0.0))
        table_ref[s, 3 * count : 4 * count, :] = table
        inputs = mm(table, tokens_ref[...], TN)
        seeds = mm(pieces(jnp.where(here, scale_at, 0.0)), cots, TN)
        for c in range(2):
            at = slice(c * LANE, (c + 1) * LANE)
            rows_ref[pl.ds(s * 4 + c, peers, stride=TILE), :] = inputs[:, at]
            rows_ref[pl.ds(s * 4 + 2 + c, peers, stride=TILE), :] = seeds[:, at]
    send_ref[...] = rows_ref[...].astype(bf16)


def gather_kernel(gate_ref, up_ref, down_ref, out_ref):
    width = gate_ref.shape[0]
    out_ref[0:width, :] = gate_ref[...]
    out_ref[width : 2 * width, :] = up_ref[...]
    out_ref[2 * width : 3 * width, :] = down_ref[...].T


def partial_kernel(came_ref, w0, w1, w2, w3, x_ref, out_ref, rows_ref, stage_ref, held, sem):
    peers = came_ref.shape[0] // TILE
    blocks = peers // QUAD
    hidden = w0.shape[1]
    width = w0.shape[0] // 3
    fetches = []
    for part in range(3):
        for k, w in enumerate((w0, w1, w2, w3)):
            at = pl.ds(part * width, width)
            fetches.append(
                pltpu.make_async_copy(w.at[at, :], held.at[k, at, :], sem.at[QUAD * part + k])
            )
            fetches[-1].start()
    wide = QUAD * width
    rows_ref[...] = came_ref[...].astype(f32)
    for j in range(TILE):
        stage_ref[j] = rows_ref[pl.ds(j, peers, stride=TILE), :].astype(bf16)
    mine = me()
    for k in range(QUAD):
        at = pl.ds(pl.multiple_of((mine ^ k) * blocks, blocks), blocks)
        for s in range(SLOTS):
            for c in range(4):
                column = (c // 2) * wide + k * width + (c % 2) * LANE
                x_ref[s * blocks : (s + 1) * blocks, column : column + LANE] = stage_ref[
                    s * 4 + c, at, :
                ]
    for part in range(3):
        total = jnp.zeros((SLOTS * blocks, hidden), f32)
        for k in range(QUAD):
            column = (part // 2) * wide + k * width
            fetches[QUAD * part + k].wait()
            total = total + mm(
                x_ref[:, column : column + width],
                held[k, part * width : (part + 1) * width, :],
                NN,
            )
        out_ref[:, part * hidden : (part + 1) * hidden] = total.astype(bf16)


def middle_kernel(parts_ref, out_ref):
    groups, rows, wide = parts_ref.shape
    hidden = wide // 3
    total = parts_ref[0].astype(f32)
    for g in range(1, groups):
        total = total + parts_ref[g].astype(f32)
    gate_sum = total[:, 0:hidden]
    up_sum = total[:, hidden : 2 * hidden]
    hidden_cot = total[:, 2 * hidden : 3 * hidden]
    sigmoid = 1.0 / (1.0 + jnp.exp(-gate_sum))
    active = gate_sum * sigmoid
    slopes = sigmoid * (1.0 + gate_sum * (1.0 - sigmoid))
    inner = (active * up_sum).astype(bf16)
    gate_cot = (hidden_cot * up_sum * slopes).astype(bf16)
    up_cot = (hidden_cot * active).astype(bf16)
    for g in range(groups):
        out_ref[g, :, 0:hidden] = inner
        out_ref[g, :, hidden : 2 * hidden] = gate_cot
        out_ref[g, :, 2 * hidden : 3 * hidden] = up_cot


def back_kernel(hgu_ref, w0, w1, w2, w3, send_ref, stage_ref, rows_ref, held, sem):
    hidden = w0.shape[1]
    width = w0.shape[0] // 3
    fetches = []
    for k, w in enumerate((w0, w1, w2, w3)):
        for part in range(3):
            at = pl.ds(part * width, width)
            fetches.append(
                pltpu.make_async_copy(w.at[at, :], held.at[k, at, :], sem.at[3 * k + part])
            )
            fetches[-1].start()
    blocks = hgu_ref.shape[0] // SLOTS
    peers = QUAD * blocks
    mine = me()
    inner = hgu_ref[:, 0:hidden]
    gate_cot = hgu_ref[:, hidden : 2 * hidden]
    up_cot = hgu_ref[:, 2 * hidden : 3 * hidden]
    for k in range(QUAD):
        for fetch in fetches[3 * k : 3 * k + 3]:
            fetch.wait()
        out = mm(inner, held[k, 2 * width : 3 * width, :], NT)
        back = mm(gate_cot, held[k, 0:width, :], NT) + mm(
            up_cot, held[k, width : 2 * width, :], NT
        )
        at = pl.ds(pl.multiple_of((mine ^ k) * blocks, blocks), blocks)
        for s in range(SLOTS):
            rows = slice(s * blocks, (s + 1) * blocks)
            for c in range(2):
                lanes = slice(c * LANE, (c + 1) * LANE)
                stage_ref[s * 4 + c, at, :] = out[rows, lanes]
                stage_ref[s * 4 + 2 + c, at, :] = back[rows, lanes]
    for j in range(TILE):
        rows_ref[pl.ds(j, peers, stride=TILE), :] = stage_ref[j]
    send_ref[...] = rows_ref[...].astype(bf16)


def grads_kernel(x_ref, hgu_ref, keep_ref, send_ref, made, sem):
    hidden = hgu_ref.shape[1] // 3
    width = keep_ref.shape[1] // 3
    wide = QUAD * width
    writes = []
    for k in (1, 3, 0, 2):
        out_ref = send_ref if k % 2 else keep_ref
        for part, (column, factor) in enumerate(((0, 1), (0, 2), (1, 0))):
            start = column * wide + k * width
            at = pl.ds(part * width, width)
            made[k, at, :] = mm(
                x_ref[:, start : start + width],
                hgu_ref[:, factor * hidden : (factor + 1) * hidden],
                TN,
            ).astype(bf16)
            writes.append(
                pltpu.make_async_copy(
                    made.at[k, at, :], out_ref.at[k // 2, at, :], sem.at[len(writes)]
                )
            )
            writes[-1].start()
    for write in writes:
        write.wait()


def first_sum_kernel(keep_ref, came_ref, own_ref, other_ref):
    own_ref[...] = (keep_ref[0].astype(f32) + came_ref[0].astype(f32)).astype(bf16)
    other_ref[...] = (keep_ref[1].astype(f32) + came_ref[1].astype(f32)).astype(bf16)


def last_sum_kernel(own_ref, came_ref, gate_ref, up_ref, down_ref):
    width = gate_ref.shape[0]

    def total(part):
        at = slice(part * width, (part + 1) * width)
        return (own_ref[at, :].astype(f32) + came_ref[at, :].astype(f32)).astype(bf16)

    gate_ref[...] = total(0)
    up_ref[...] = total(1)
    down_ref[...] = total(2).T


def combine_kernel(table_ref, came_ref, out_ref, grad_ref, rows_ref):
    count, width = out_ref.shape
    peers = came_ref.shape[0] // TILE
    rows_ref[...] = came_ref[...].astype(f32)

    def picked(s, c):
        return jnp.concatenate(
            [rows_ref[pl.ds(s * 4 + c + i, peers, stride=TILE), :] for i in range(2)], axis=1
        ).astype(bf16)

    parts = jnp.zeros((3 * count, width), f32)
    grad = jnp.zeros((count, width), f32)
    for s in range(SLOTS):
        parts = parts + mm(table_ref[s, 0 : 3 * count, :], picked(s, 0), NN)
        grad = grad + mm(table_ref[s, 3 * count : 4 * count, :], picked(s, 2), NN)
    out_ref[...] = (
        parts[0:count] + parts[count : 2 * count] + parts[2 * count : 3 * count]
    ).astype(bf16)
    grad_ref[...] = grad.astype(bf16)


def local(
    tokens, cotangent, route_probs, expert_ids, seq_ids, ratios, gate_weight, up_weight, down_weight
):
    count, width = tokens.shape
    hidden = gate_weight.shape[2]
    sources = lax.axis_size("replica")
    others = ("xh", "yh")
    groups = lax.axis_size("xh") * lax.axis_size("yh")
    peers = QUAD * sources
    rows = SLOTS * sources
    shape = jax.ShapeDtypeStruct
    message = shape((peers * TILE, LANE), bf16)
    everyone = ("yl", "core", "replica")
    flip = [(0, 1), (1, 0)]
    product = 2 * rows * QUAD * width * hidden
    weight_bytes = 2 * 3 * QUAD * width * hidden

    def spread(x, axis):
        return lax.all_to_all(x, axis, split_axis=0, concat_axis=0, tiled=True)

    def messages(x):
        return spread(x.reshape(peers, TILE, LANE), everyone).reshape(peers * TILE, LANE)

    arrays = (
        tokens,
        cotangent,
        route_probs.T,
        expert_ids.T,
        seq_ids.reshape(1, count),
        ratios.reshape(1, -1),
    )
    send, table = call(
        pack_kernel,
        (message, shape((SLOTS, 4 * count, peers), bf16)),
        16 * peers * count * width,
        4 * peers * TILE * LANE,
        60,
        in_specs=[pl.BlockSpec(memory_space=pl.ANY)] * len(arrays),
        scratch_shapes=[pltpu.VMEM((peers * TILE, LANE), f32)]
        + [pltpu.VMEM(a.shape, a.dtype) for a in arrays]
        + [pltpu.SemaphoreType.DMA((len(arrays),))],
    )(*arrays)
    came = messages(send)

    w0 = call(gather_kernel, shape((3 * width, hidden), bf16), 0, 12 * width * hidden, ROOM)(
        gate_weight[0], up_weight[0], down_weight[0]
    )
    w2 = lax.ppermute(w0, "yl", flip)
    w1 = lax.ppermute(w0, "core", flip)
    w3 = lax.ppermute(w2, "core", flip)

    x, partial = call(
        partial_kernel,
        (shape((rows, 2 * QUAD * width), bf16), shape((rows, 3 * hidden), bf16)),
        3 * product,
        weight_bytes,
        ROOM,
        in_specs=[pl.BlockSpec(memory_space=pltpu.VMEM)]
        + [pl.BlockSpec(memory_space=pl.ANY)] * QUAD,
        scratch_shapes=[
            pltpu.VMEM((peers * TILE, LANE), f32),
            pltpu.VMEM((TILE, peers, LANE), bf16),
            pltpu.VMEM((QUAD, 3 * width, hidden), bf16),
            pltpu.SemaphoreType.DMA((3 * QUAD,)),
        ],
    )(came, w0, w1, w2, w3)
    parts = spread(partial.reshape(groups, rows // groups, 3 * hidden), others)
    copies = call(
        middle_kernel,
        shape((groups, rows // groups, 3 * hidden), bf16),
        20 * rows * 3 * hidden,
        4 * rows * 3 * hidden,
    )(parts)
    hgu = spread(copies, others).reshape(rows, 3 * hidden)
    sent_back = call(
        back_kernel,
        message,
        3 * product,
        weight_bytes,
        ROOM,
        in_specs=[pl.BlockSpec(memory_space=pltpu.VMEM)]
        + [pl.BlockSpec(memory_space=pl.ANY)] * QUAD,
        scratch_shapes=[
            pltpu.VMEM((TILE, peers, LANE), f32),
            pltpu.VMEM((peers * TILE, LANE), f32),
            pltpu.VMEM((QUAD, 3 * width, hidden), bf16),
            pltpu.SemaphoreType.DMA((3 * QUAD,)),
        ],
    )(hgu, w0, w1, w2, w3)

    pair = shape((2, 3 * width, hidden), bf16)
    one = shape((3 * width, hidden), bf16)
    returned = messages(sent_back)
    keep, give = call(
        grads_kernel,
        (pair, pair),
        3 * product,
        weight_bytes,
        LARGE,
        out_specs=[pl.BlockSpec(memory_space=pl.ANY)] * 2,
        scratch_shapes=[
            pltpu.VMEM((QUAD, 3 * width, hidden), bf16),
            pltpu.SemaphoreType.DMA((3 * QUAD,)),
        ],
    )(x, hgu)
    got = lax.ppermute(give, "core", flip)
    own, other = call(
        first_sum_kernel,
        (one, one),
        6 * width * hidden,
        2 * weight_bytes,
        LARGE,
        grid=(6,),
        in_specs=[pl.BlockSpec((2, width // 2, hidden), lambda i: (0, i, 0))] * 2,
        out_specs=[pl.BlockSpec((width // 2, hidden), lambda i: (i, 0))] * 2,
    )(keep, got)
    theirs = lax.ppermute(other, "yl", flip)
    grads = call(
        last_sum_kernel,
        (
            shape((width, hidden), bf16),
            shape((width, hidden), bf16),
            shape((hidden, width), bf16),
        ),
        3 * width * hidden,
        weight_bytes,
    )(own, theirs)
    layer_out, grad_tokens = call(
        combine_kernel,
        (shape((count, width), bf16), shape((count, width), bf16)),
        16000 * peers * count * width,
        4 * peers * TILE * LANE,
        scratch_shapes=[pltpu.VMEM((peers * TILE, LANE), f32)],
    )(table, returned)
    return (layer_out, grad_tokens) + tuple(g[None] for g in grads)


def solution(mesh):
    axes = ("yh", "yl", "xh", "core")
    shape = (mesh.shape["expert"] // 8, 2, 2, 2, mesh.shape["replica"])
    quads = Mesh(mesh.devices.reshape(shape), axes + ("replica",))
    expert = axes
    return jax.shard_map(
        local,
        mesh=quads,
        in_specs=(
            P("replica", expert),
            P("replica", expert),
            P("replica", None),
            P("replica", None),
            P("replica"),
            P(),
            P("replica", expert, None),
            P("replica", expert, None),
            P("replica", None, expert),
        ),
        out_specs=(
            P("replica", expert),
            P("replica", expert),
            P("replica", expert, None),
            P("replica", expert, None),
            P("replica", None, expert),
        ),
        check_vma=False,
    )
```

```python
import jax
import jax.numpy as jnp
from jax import lax
from jax.experimental import pallas as pl
from jax.experimental.pallas import tpu as pltpu
from jax.sharding import Mesh
from jax.sharding import PartitionSpec as P

clip_low = 0.8
clip_high = 1.25

bf16 = jnp.bfloat16
f32 = jnp.float32

NN = (((1,), (0,)), ((), ()))
NT = (((1,), (1,)), ((), ()))
TN = (((0,), (0,)), ((), ()))

QUAD = 4
SLOTS = 2
TILE = 8
LANE = 128
ROOM = 50
LARGE = 60


def mm(a, b, dims):
    return lax.dot_general(a, b, dims, preferred_element_type=f32)


def call(body, outs, flops, nbytes, room=24, **more):
    return pl.pallas_call(
        body,
        out_shape=outs,
        cost_estimate=pl.CostEstimate(flops=flops, bytes_accessed=nbytes, transcendentals=0),
        compiler_params=pltpu.CompilerParams(vmem_limit_bytes=room * 1024 * 1024),
        **more,
    )


def me():
    return lax.axis_index("xh") * 2 + lax.axis_index("core")


def pieces(x):
    first = x.astype(bf16)
    rest = x - first.astype(f32)
    second = rest.astype(bf16)
    third = (rest - second.astype(f32)).astype(bf16)
    return jnp.concatenate([first, second, third], axis=0)


def pack_kernel(*refs):
    arrays, (send_ref, table_ref, rows_ref), held, sem = refs[:6], refs[6:9], refs[9:15], refs[15]
    copies = [pltpu.make_async_copy(a, b, sem.at[i]) for i, (a, b) in enumerate(zip(arrays, held))]
    for copy in copies:
        copy.start()
    for copy in copies:
        copy.wait()
    tokens_ref, cot_ref, probs_ref, ids_ref, seq_ref, ratios_ref = held
    count, width = tokens_ref.shape
    routes = ids_ref.shape[0]
    peers = send_ref.shape[0] // TILE
    experts = peers // QUAD
    down = lax.broadcasted_iota(jnp.int32, (count, count), 0)
    across = lax.broadcasted_iota(jnp.int32, (count, count), 1)

    def column(row):
        return jnp.sum(jnp.where(down == across, row, 0.0), axis=1, keepdims=True)

    labels = lax.broadcasted_iota(jnp.int32, (count, ratios_ref.shape[1]), 1).astype(f32)
    same = labels == column(seq_ref[...].astype(f32))
    picked = jnp.sum(jnp.where(same, ratios_ref[...], 0.0), axis=1, keepdims=True)
    weights = jnp.clip(picked, clip_low, clip_high)
    ids = ids_ref[...].astype(f32)
    peer = lax.broadcasted_iota(jnp.int32, (count, peers), 1)
    owner = lax.rem(peer, experts).astype(f32)
    first_slot = (lax.div(peer, experts) * SLOTS).astype(f32)
    member = jnp.zeros((count, peers), f32)
    prob_at = jnp.zeros((count, peers), f32)
    for k in range(routes):
        named = column(ids[k : k + 1, :]) == owner
        member = jnp.where(named, 1.0, member)
        prob_at = jnp.where(named, column(probs_ref[k : k + 1, :]), prob_at)
    scale_at = prob_at * weights
    lower = jnp.where(down > across, 1.0, 0.0).astype(bf16)
    before = mm(lower, member.astype(bf16), NN)
    cot = cot_ref[...]
    cots = jnp.concatenate([cot, cot, cot], axis=0)
    for s in range(SLOTS):
        here = (member > 0.0) & (before == first_slot + s)
        table = jnp.where(here, 1.0, 0.0).astype(bf16)
        table_ref[s, 0 : 3 * count, :] = pieces(jnp.where(here, prob_at, 0.0))
        table_ref[s, 3 * count : 4 * count, :] = table
        inputs = mm(table, tokens_ref[...], TN)
        seeds = mm(pieces(jnp.where(here, scale_at, 0.0)), cots, TN)
        for c in range(2):
            at = slice(c * LANE, (c + 1) * LANE)
            rows_ref[pl.ds(s * 4 + c, peers, stride=TILE), :] = inputs[:, at]
            rows_ref[pl.ds(s * 4 + 2 + c, peers, stride=TILE), :] = seeds[:, at]
    send_ref[...] = rows_ref[...].astype(bf16)


def gather_kernel(gate_ref, up_ref, down_ref, out_ref):
    width = gate_ref.shape[0]
    out_ref[0:width, :] = gate_ref[...]
    out_ref[width : 2 * width, :] = up_ref[...]
    out_ref[2 * width : 3 * width, :] = down_ref[...].T


def partial_kernel(came_ref, w0, w1, w2, w3, x_ref, out_ref, rows_ref, stage_ref, held, sem):
    peers = came_ref.shape[0] // TILE
    blocks = peers // QUAD
    hidden = w0.shape[1]
    width = w0.shape[0] // 3
    fetches = []
    for part in range(3):
        for k, w in enumerate((w0, w1, w2, w3)):
            at = pl.ds(part * width, width)
            fetches.append(
                pltpu.make_async_copy(w.at[at, :], held.at[k, at, :], sem.at[QUAD * part + k])
            )
            fetches[-1].start()
    wide = QUAD * width
    rows_ref[...] = came_ref[...].astype(f32)
    for j in range(TILE):
        stage_ref[j] = rows_ref[pl.ds(j, peers, stride=TILE), :].astype(bf16)
    mine = me()
    for k in range(QUAD):
        at = pl.ds(pl.multiple_of((mine ^ k) * blocks, blocks), blocks)
        for s in range(SLOTS):
            for c in range(4):
                column = (c // 2) * wide + k * width + (c % 2) * LANE
                x_ref[s * blocks : (s + 1) * blocks, column : column + LANE] = stage_ref[
                    s * 4 + c, at, :
                ]
    for part in range(3):
        total = jnp.zeros((SLOTS * blocks, hidden), f32)
        for k in range(QUAD):
            column = (part // 2) * wide + k * width
            fetches[QUAD * part + k].wait()
            total = total + mm(
                x_ref[:, column : column + width],
                held[k, part * width : (part + 1) * width, :],
                NN,
            )
        out_ref[:, part * hidden : (part + 1) * hidden] = total.astype(bf16)


def middle_kernel(parts_ref, out_ref):
    groups, rows, wide = parts_ref.shape
    hidden = wide // 3
    total = parts_ref[0].astype(f32)
    for g in range(1, groups):
        total = total + parts_ref[g].astype(f32)
    gate_sum = total[:, 0:hidden]
    up_sum = total[:, hidden : 2 * hidden]
    hidden_cot = total[:, 2 * hidden : 3 * hidden]
    sigmoid = 1.0 / (1.0 + jnp.exp(-gate_sum))
    active = gate_sum * sigmoid
    slopes = sigmoid * (1.0 + gate_sum * (1.0 - sigmoid))
    inner = (active * up_sum).astype(bf16)
    gate_cot = (hidden_cot * up_sum * slopes).astype(bf16)
    up_cot = (hidden_cot * active).astype(bf16)
    for g in range(groups):
        out_ref[g, :, 0:hidden] = inner
        out_ref[g, :, hidden : 2 * hidden] = gate_cot
        out_ref[g, :, 2 * hidden : 3 * hidden] = up_cot


def back_kernel(hgu_ref, w0, w1, w2, w3, send_ref, stage_ref, rows_ref):
    hidden = w0.shape[1]
    width = w0.shape[0] // 3
    blocks = hgu_ref.shape[0] // SLOTS
    peers = QUAD * blocks
    mine = me()
    inner = hgu_ref[:, 0:hidden]
    gate_cot = hgu_ref[:, hidden : 2 * hidden]
    up_cot = hgu_ref[:, 2 * hidden : 3 * hidden]
    for k, w in enumerate((w0, w1, w2, w3)):
        out = mm(inner, w[2 * width : 3 * width, :], NT)
        back = mm(gate_cot, w[0:width, :], NT) + mm(
            up_cot, w[width : 2 * width, :], NT
        )
        at = pl.ds(pl.multiple_of((mine ^ k) * blocks, blocks), blocks)
        for s in range(SLOTS):
            rows = slice(s * blocks, (s + 1) * blocks)
            for c in range(2):
                lanes = slice(c * LANE, (c + 1) * LANE)
                stage_ref[s * 4 + c, at, :] = out[rows, lanes]
                stage_ref[s * 4 + 2 + c, at, :] = back[rows, lanes]
    for j in range(TILE):
        rows_ref[pl.ds(j, peers, stride=TILE), :] = stage_ref[j]
    send_ref[...] = rows_ref[...].astype(bf16)


def grads_kernel(x_ref, hgu_ref, keep_ref, send_ref, made, sem):
    hidden = hgu_ref.shape[1] // 3
    width = keep_ref.shape[1] // 3
    wide = QUAD * width
    writes = []
    for k in (1, 3, 0, 2):
        out_ref = send_ref if k % 2 else keep_ref
        for part, (column, factor) in enumerate(((0, 1), (0, 2), (1, 0))):
            start = column * wide + k * width
            at = pl.ds(part * width, width)
            made[k, at, :] = mm(
                x_ref[:, start : start + width],
                hgu_ref[:, factor * hidden : (factor + 1) * hidden],
                TN,
            ).astype(bf16)
            writes.append(
                pltpu.make_async_copy(
                    made.at[k, at, :], out_ref.at[k // 2, at, :], sem.at[len(writes)]
                )
            )
            writes[-1].start()
    for write in writes:
        write.wait()


def first_sum_kernel(keep_ref, came_ref, own_ref, other_ref):
    own_ref[...] = (keep_ref[0].astype(f32) + came_ref[0].astype(f32)).astype(bf16)
    other_ref[...] = (keep_ref[1].astype(f32) + came_ref[1].astype(f32)).astype(bf16)


def last_sum_kernel(own_ref, came_ref, gate_ref, up_ref, down_ref):
    width = gate_ref.shape[0]

    def total(part):
        at = slice(part * width, (part + 1) * width)
        return (own_ref[at, :].astype(f32) + came_ref[at, :].astype(f32)).astype(bf16)

    gate_ref[...] = total(0)
    up_ref[...] = total(1)
    down_ref[...] = total(2).T


def combine_kernel(table_ref, came_ref, out_ref, grad_ref, rows_ref):
    count, width = out_ref.shape
    peers = came_ref.shape[0] // TILE
    rows_ref[...] = came_ref[...].astype(f32)

    def picked(s, c):
        return jnp.concatenate(
            [rows_ref[pl.ds(s * 4 + c + i, peers, stride=TILE), :] for i in range(2)], axis=1
        ).astype(bf16)

    parts = jnp.zeros((3 * count, width), f32)
    grad = jnp.zeros((count, width), f32)
    for s in range(SLOTS):
        parts = parts + mm(table_ref[s, 0 : 3 * count, :], picked(s, 0), NN)
        grad = grad + mm(table_ref[s, 3 * count : 4 * count, :], picked(s, 2), NN)
    out_ref[...] = (
        parts[0:count] + parts[count : 2 * count] + parts[2 * count : 3 * count]
    ).astype(bf16)
    grad_ref[...] = grad.astype(bf16)


def local(
    tokens, cotangent, route_probs, expert_ids, seq_ids, ratios, gate_weight, up_weight, down_weight
):
    count, width = tokens.shape
    hidden = gate_weight.shape[2]
    sources = lax.axis_size("replica")
    others = ("yh", "yl")
    groups = lax.axis_size("yh") * lax.axis_size("yl")
    peers = QUAD * sources
    rows = SLOTS * sources
    shape = jax.ShapeDtypeStruct
    message = shape((peers * TILE, LANE), bf16)
    everyone = ("xh", "core", "replica")
    flip = [(0, 1), (1, 0)]
    product = 2 * rows * QUAD * width * hidden
    weight_bytes = 2 * 3 * QUAD * width * hidden

    def spread(x, axis):
        return lax.all_to_all(x, axis, split_axis=0, concat_axis=0, tiled=True)

    def messages(x):
        return spread(x.reshape(peers, TILE, LANE), everyone).reshape(peers * TILE, LANE)

    arrays = (
        tokens,
        cotangent,
        route_probs.T,
        expert_ids.T,
        seq_ids.reshape(1, count),
        ratios.reshape(1, -1),
    )
    send, table = call(
        pack_kernel,
        (message, shape((SLOTS, 4 * count, peers), bf16)),
        16 * peers * count * width,
        4 * peers * TILE * LANE,
        60,
        in_specs=[pl.BlockSpec(memory_space=pl.ANY)] * len(arrays),
        scratch_shapes=[pltpu.VMEM((peers * TILE, LANE), f32)]
        + [pltpu.VMEM(a.shape, a.dtype) for a in arrays]
        + [pltpu.SemaphoreType.DMA((len(arrays),))],
    )(*arrays)
    came = messages(send)

    w0 = call(gather_kernel, shape((3 * width, hidden), bf16), 0, 12 * width * hidden, ROOM)(
        gate_weight[0], up_weight[0], down_weight[0]
    )
    w2 = lax.ppermute(w0, "xh", flip)
    w1 = lax.ppermute(w0, "core", flip)
    w3 = lax.ppermute(w2, "core", flip)

    x, partial = call(
        partial_kernel,
        (shape((rows, 2 * QUAD * width), bf16), shape((rows, 3 * hidden), bf16)),
        3 * product,
        weight_bytes,
        ROOM,
        in_specs=[pl.BlockSpec(memory_space=pltpu.VMEM)]
        + [pl.BlockSpec(memory_space=pl.ANY)] * QUAD,
        scratch_shapes=[
            pltpu.VMEM((peers * TILE, LANE), f32),
            pltpu.VMEM((TILE, peers, LANE), bf16),
            pltpu.VMEM((QUAD, 3 * width, hidden), bf16),
            pltpu.SemaphoreType.DMA((3 * QUAD,)),
        ],
    )(came, w0, w1, w2, w3)
    parts = spread(partial.reshape(groups, rows // groups, 3 * hidden), others)
    copies = call(
        middle_kernel,
        shape((groups, rows // groups, 3 * hidden), bf16),
        20 * rows * 3 * hidden,
        4 * rows * 3 * hidden,
    )(parts)
    hgu = spread(copies, others).reshape(rows, 3 * hidden)
    sent_back = call(
        back_kernel,
        message,
        3 * product,
        weight_bytes,
        scratch_shapes=[
            pltpu.VMEM((TILE, peers, LANE), f32),
            pltpu.VMEM((peers * TILE, LANE), f32),
        ],
    )(hgu, w0, w1, w2, w3)

    pair = shape((2, 3 * width, hidden), bf16)
    one = shape((3 * width, hidden), bf16)
    returned = messages(sent_back)
    keep, give = call(
        grads_kernel,
        (pair, pair),
        3 * product,
        weight_bytes,
        LARGE,
        out_specs=[pl.BlockSpec(memory_space=pl.ANY)] * 2,
        scratch_shapes=[
            pltpu.VMEM((QUAD, 3 * width, hidden), bf16),
            pltpu.SemaphoreType.DMA((3 * QUAD,)),
        ],
    )(x, hgu)
    got = lax.ppermute(give, "core", flip)
    own, other = call(
        first_sum_kernel,
        (one, one),
        6 * width * hidden,
        2 * weight_bytes,
        LARGE,
        grid=(6,),
        in_specs=[pl.BlockSpec((2, width // 2, hidden), lambda i: (0, i, 0))] * 2,
        out_specs=[pl.BlockSpec((width // 2, hidden), lambda i: (i, 0))] * 2,
    )(keep, got)
    theirs = lax.ppermute(other, "xh", flip)
    grads = call(
        last_sum_kernel,
        (
            shape((width, hidden), bf16),
            shape((width, hidden), bf16),
            shape((hidden, width), bf16),
        ),
        3 * width * hidden,
        weight_bytes,
    )(own, theirs)
    layer_out, grad_tokens = call(
        combine_kernel,
        (shape((count, width), bf16), shape((count, width), bf16)),
        16000 * peers * count * width,
        4 * peers * TILE * LANE,
        scratch_shapes=[pltpu.VMEM((peers * TILE, LANE), f32)],
    )(table, returned)
    return (layer_out, grad_tokens) + tuple(g[None] for g in grads)


def solution(mesh):
    axes = ("yh", "yl", "xh", "core")
    shape = (mesh.shape["expert"] // 8, 2, 2, 2, mesh.shape["replica"])
    quads = Mesh(mesh.devices.reshape(shape), axes + ("replica",))
    expert = axes
    return jax.shard_map(
        local,
        mesh=quads,
        in_specs=(
            P("replica", expert),
            P("replica", expert),
            P("replica", None),
            P("replica", None),
            P("replica"),
            P(),
            P("replica", expert, None),
            P("replica", expert, None),
            P("replica", None, expert),
        ),
        out_specs=(
            P("replica", expert),
            P("replica", expert),
            P("replica", expert, None),
            P("replica", expert, None),
            P("replica", None, expert),
        ),
        check_vma=False,
    )
```
